512 devices in a mesh: pencil: 32 (over z, x_lo, core), slab: 16 (over y, x_hi).
Axes of the slice: x: 4 (x_hi: 2, x_lo: 2; x = x_hi * 2 + x_lo), y: 8, z: 8, core: 2. Of those that a mesh axis runs over, the one named last changes fastest.
Arguments:
- strain: bfloat16 [6, 16, 512, 2048], P(None, None, 'pencil', 'slab'), may hold values from -6 to 6
- labels: int32 [16, 512, 2048], P(None, 'pencil', 'slab'), may hold values from 0 to 3
- moduli: float32 [2, 4], replicated, may hold values from 0.05 to 4
Outputs:
- strain_band: float32 [6, 2, 2, 512, 2048], P(None, None, None, 'pencil', 'slab')
The draws below stay inside these ranges and needn't reach their ends.
All inputs are finite; a program needn't handle non-finite values.
Results may differ from the reference program's by a relative error of at most 0.022.
Values may be sent and summed in bfloat16 or wider, within the bound.
A program may use at most 128 MiB of HBM per device.

```python
import math
import jax
import jax.numpy as jnp
from jax import lax

NX = 2048
XW = 16
MODES = 2
KX0 = 64
NPHASE = 4
NY = 512
NZ = 2048


def touch_ends(values, rng, smallest, largest):
    longest = values.shape.index(max(values.shape))
    spots = []
    for shift in (0, 1):
        where = [jax.random.randint(jax.random.fold_in(rng, axis), (), 0, length) for axis, length in enumerate(values.shape)]
        where[longest] = (where[longest] + shift) % values.shape[longest]
        spots.append(tuple(where))
    return values.at[spots[0]].set(smallest).at[spots[1]].set(largest)


def steps_of(key, shape, pieces, smallest, high):
    level, own = 1.0, jax.random.fold_in(key, 6)
    for position, parts in pieces:
        heights = jnp.exp(jax.random.uniform(jax.random.fold_in(own, position), (parts,), jnp.float32, smallest / len(pieces), high / len(pieces)))
        level = level * jnp.repeat(heights, shape[position] // parts).reshape([-1 if axis == position else 1 for axis in range(len(shape))])
    return level


def noise(own_key, extent, spread, bound, split=(), held_as=jnp.bfloat16):
    array = spread * jax.random.normal(own_key, extent, jnp.float32)
    if split:
        array = array * steps_of(own_key, extent, split, -0.22, 0.18)
    return jnp.clip(array, -bound, bound).astype(held_as)


def setup_inputs(seed: int = 0) -> dict:
    splits = jax.random.split(jax.random.key(seed), 4)
    return {
        "strain": noise(splits[0], (6, XW, NY, NZ), 1.0, 6.0, ((2, 32), (3, 16))),
        "labels": touch_ends(jax.random.randint(splits[1], (XW, NY, NZ), 0, NPHASE), jax.random.fold_in(splits[1], 1), 0, NPHASE - 1).astype(jnp.int32),
        "moduli": jnp.clip(jnp.exp(jax.random.uniform(splits[2], (2, NPHASE), jnp.float32, math.log(0.05), math.log(4.0))), 0.05, 4.0),
    }


q_floor = 0.01

def reference_medium(moduli):
    lam0 = 0.5 * (jnp.min(moduli[0]) + jnp.max(moduli[0]))
    mu0 = 0.5 * (jnp.min(moduli[1]) + jnp.max(moduli[1]))
    return (lam0, mu0)

def green(spectrum, qx, qy, qz, lam0, mu0):
    txx, tyy, tzz = (spectrum[0], spectrum[1], spectrum[2])
    tyz, txz, txy = (spectrum[3], spectrum[4], spectrum[5])
    vecx = txx * qx + txy * qy + txz * qz
    vecy = txy * qx + tyy * qy + tyz * qz
    vecz = txz * qx + tyz * qy + tzz * qz
    inner = qx * vecx + qy * vecy + qz * vecz
    square = jnp.maximum(qx * qx + qy * qy + qz * qz, q_floor)
    factor = (lam0 + mu0) / (mu0 * (lam0 + 2.0 * mu0))
    first = 1.0 / (2.0 * mu0 * square)
    second = factor * inner / (square * square)
    out_xx = -(first * (2.0 * qx * vecx) - second * qx * qx)
    out_yy = -(first * (2.0 * qy * vecy) - second * qy * qy)
    out_zz = -(first * (2.0 * qz * vecz) - second * qz * qz)
    out_yz = -(first * (qy * vecz + qz * vecy) - second * qy * qz)
    out_xz = -(first * (qx * vecz + qz * vecx) - second * qx * qz)
    out_xy = -(first * (qx * vecy + qy * vecx) - second * qx * qy)
    return jnp.stack([out_xx, out_yy, out_zz, out_yz, out_xz, out_xy], 0)

def frequencies(kx, ky, kz, size_x, size_y, size_z):
    angle_x = kx.astype(jnp.float32) * (math.pi / size_x)
    angle_y = ky.astype(jnp.float32) * (math.pi / size_y)
    angle_z = kz.astype(jnp.float32) * (math.pi / size_z)
    sin_x = jnp.sin(angle_x)[:, None, None]
    cos_x = jnp.cos(angle_x)[:, None, None]
    sin_y = jnp.sin(angle_y)[None, :, None]
    cos_y = jnp.cos(angle_y)[None, :, None]
    sin_z = jnp.sin(angle_z)[None, None, :]
    cos_z = jnp.cos(angle_z)[None, None, :]
    return (sin_x * cos_y * cos_z, cos_x * sin_y * cos_z, cos_x * cos_y * sin_z)

def reference(strain, labels, moduli):
    lam0, mu0 = reference_medium(moduli)
    shift_lam = jnp.zeros(labels.shape, jnp.float32)
    shift_mu = jnp.zeros(labels.shape, jnp.float32)
    for phase in range(NPHASE):
        hit = labels == phase
        shift_lam = jnp.where(hit, moduli[0, phase] - lam0, shift_lam)
        shift_mu = jnp.where(hit, moduli[1, phase] - mu0, shift_mu)
    trace = strain[0].astype(jnp.float32) + strain[1].astype(jnp.float32) + strain[2].astype(jnp.float32)
    kx = KX0 + jnp.arange(MODES, dtype=jnp.int32)
    planes = jnp.arange(XW, dtype=jnp.int32)
    product = kx[:, None] * planes[None, :] % NX
    angle = product.astype(jnp.float32) * (2.0 * math.pi / NX)
    scale = 1.0 / math.sqrt(XW)
    table = jnp.stack([jnp.cos(angle) * scale, -jnp.sin(angle) * scale], 0)
    bands = []
    for comp in range(6):
        values = strain[comp].astype(jnp.float32)
        if comp < 3:
            term = shift_lam * trace + 2.0 * shift_mu * values
        else:
            term = 2.0 * shift_mu * values
        rounded = lax.optimization_barrier(term.astype(jnp.bfloat16))
        bands.append(jnp.einsum('rmx,xyz->rmyz', table, rounded.astype(jnp.float32), precision=lax.Precision.HIGHEST))
    x_band = jnp.stack(bands, 0).astype(jnp.bfloat16)
    complex_x = lax.complex(x_band[:, 0].astype(jnp.float32), x_band[:, 1].astype(jnp.float32))
    complex_y = jnp.fft.fft(complex_x, axis=2) / math.sqrt(NY)
    y_real = jnp.real(complex_y).astype(jnp.bfloat16).astype(jnp.float32)
    y_imag = jnp.imag(complex_y).astype(jnp.bfloat16).astype(jnp.float32)
    complex_z = jnp.fft.fft(lax.complex(y_real, y_imag), axis=3) / math.sqrt(NZ)
    z_band = jnp.stack([jnp.real(complex_z), jnp.imag(complex_z)], 1).astype(jnp.float32)
    qx, qy, qz = frequencies(kx, jnp.arange(NY, dtype=jnp.int32), jnp.arange(NZ, dtype=jnp.int32), NX, NY, NZ)
    return green(z_band, qx[None], qy[None], qz[None], lam0, mu0)
```

```python
import math

import jax
import jax.numpy as jnp
import numpy as np
from jax import lax
from jax.experimental import pallas as pl
from jax.experimental.pallas import tpu as pltpu
from jax.sharding import PartitionSpec as P

MESH = pl.DeviceIdType.MESH
NX, NY, NZ = 2048, 512, 2048
XW, MODES, KX0, NPHASE, COMPS = 16, 2, 64, 4, 6
PENCIL, SLAB = 32, 16
UNITS_Y, UNITS_Z = 24, 12
Q_FLOOR = 0.01
F32, BF16 = jnp.float32, jnp.bfloat16


def unit_place(unit):
    return unit // 3 * 4 + unit % 3


def place_unit(place):
    return place // 4 * 3 + place % 4


def tables():
    angle = 2 * math.pi / NY * (np.outer(np.arange(NY), np.arange(NY)) % NY)
    along_y = np.concatenate([np.cos(angle), np.sin(angle)], 1)
    angle = 2 * math.pi / 32 * (np.outer(np.arange(32), np.arange(32)) % 32)
    same = np.eye(16)
    coarse = [np.einsum("bt,kj->kbtj", f(angle), same).reshape(512, 512) for f in (np.cos, np.sin)]
    coarse = np.concatenate(coarse, 1)
    angle = 2 * math.pi / NZ * np.outer(np.arange(32), np.arange(64))
    scale = 1 / math.sqrt(NZ)
    turn = np.stack([np.tile(np.cos(angle), 2), np.concatenate([np.sin(angle), -np.sin(angle)], 1)]) * scale
    angle = 2 * math.pi / 64 * (np.outer(np.arange(64), np.arange(64)) % 64)
    cosine, sine = np.cos(angle), np.sin(angle)
    fine = np.stack([np.concatenate([cosine, sine], 1), np.concatenate([-sine, cosine], 1)])
    fine = fine.reshape(2, 16, 4, 128).transpose(1, 0, 2, 3)
    fine = np.stack([np.roll(fine, -delta, 2).reshape(128, 128) for delta in range(4)])
    rows = np.arange(32)
    ky = 16 * np.arange(PENCIL)[:, None] + (rows // 8 * 4 + rows % 4)[None, :]
    angle = np.broadcast_to((math.pi / NY * ky)[:, :, None], (PENCIL, 32, 128))
    freq_y = np.stack([np.sin(angle), np.cos(angle)], 1)
    angle = math.pi / NZ * np.arange(NZ).reshape(SLAB, 1, 128)
    angle = np.broadcast_to(angle, (SLAB, 8, 128))
    freq_z = np.stack([np.sin(angle), np.cos(angle)], 1)
    return (
        along_y.astype(BF16),
        coarse.astype(BF16),
        turn.astype(np.float32),
        fine.astype(BF16),
        freq_y.astype(np.float32),
        freq_z.astype(np.float32),
    )


def swap_parts(values):
    lane = lax.broadcasted_iota(jnp.int32, values.shape, 1)
    turned = pltpu.roll(values, 64, 1)
    return jnp.where(lane < 64, turned, -turned)


def with_swapped(tile):
    return jnp.concatenate([tile, swap_parts(tile.astype(F32)).astype(BF16)], 0)


def transform_z(data, coarse, turn, fine):
    mixed = jnp.dot(coarse, with_swapped(data), preferred_element_type=F32)
    swapped = pltpu.roll(mixed, 64, 1)
    mixed = mixed.reshape(16, 32, 128) * turn[0][None] + swapped.reshape(16, 32, 128) * turn[1][None]
    mixed = mixed.reshape(512, 128).astype(BF16)
    blocks = [mixed[32 * k : 32 * k + 32] for k in range(16)]
    row = lax.broadcasted_iota(jnp.int32, (128, 512), 0)
    lane = lax.broadcasted_iota(jnp.int32, (128, 512), 1)
    shift = (lane // 32 - row) & 3
    result = None
    for delta in range(4):
        turned = jnp.concatenate([blocks[4 * (k // 4) + (k - delta) % 4] for k in range(16)], 0)
        part = lax.dot_general(fine[delta], turned, (((1,), (1,)), ((), ())), preferred_element_type=F32)
        result = part if result is None else jnp.where(shift == delta, part, result)
    return result


def contrast(labels, values, base, factor):
    levels = [(values[phase] - base) * factor for phase in range(NPHASE)]
    chosen = jnp.where(labels == 2, levels[2], levels[3])
    chosen = jnp.where(labels == 1, levels[1], chosen)
    return jnp.where(labels == 0, levels[0], chosen)


def wave(mode, plane):
    angle = 2 * math.pi / NX * ((KX0 + mode) * plane % NX)
    scale = 1 / math.sqrt(XW)
    return float(math.cos(angle) * scale), float(-math.sin(angle) * scale)


def kernel(
    moduli,
    strain_hbm,
    labels_hbm,
    along_y_hbm,
    coarse_hbm,
    turn_hbm,
    fine_hbm,
    freq_y_hbm,
    freq_z_hbm,
    out,
    strain,
    labels,
    along_y,
    coarse,
    turn,
    fine,
    freq_y,
    freq_z,
    shear,
    send1,
    land1,
    send2,
    land2,
    send3,
    land3,
    in_sems,
    table_sems,
    send_sems,
    land_sems,
):
    pencil = lax.axis_index("pencil")
    slab = lax.axis_index("slab")
    works_y = pencil % 4 < 3
    works_z = slab % 4 < 3

    loads = [
        pltpu.make_async_copy(strain_hbm, strain, in_sems.at[0]),
        pltpu.make_async_copy(labels_hbm, labels, in_sems.at[1]),
    ]
    for load in loads:
        load.start()
    pairs = [
        (freq_y_hbm.at[pencil], freq_y),
        (freq_z_hbm.at[slab], freq_z),
        (along_y_hbm, along_y),
        (coarse_hbm, coarse),
        (turn_hbm, turn),
        (fine_hbm, fine),
    ]
    table_loads = [pltpu.make_async_copy(a, b, table_sems.at[i]) for i, (a, b) in enumerate(pairs)]
    for load in table_loads:
        load.start()

    barrier = pltpu.get_barrier_semaphore()

    @pl.when(works_y)
    def _():
        def greet(step, carry):
            other = lax.rem(pencil + step, PENCIL)
            pl.semaphore_signal(barrier, inc=1, device_id=(other, slab), device_id_type=MESH)
            return carry

        lax.fori_loop(1, PENCIL, greet, 0)

    @pl.when(works_z)
    def _():
        def greet(step, carry):
            other = lax.rem(slab + step, SLAB)
            pl.semaphore_signal(barrier, inc=1, device_id=(pencil, other), device_id_type=MESH)
            return carry

        lax.fori_loop(1, SLAB, greet, 0)

    lam0 = 0.5 * (
        jnp.minimum(jnp.minimum(moduli[0, 0], moduli[0, 1]), jnp.minimum(moduli[0, 2], moduli[0, 3]))
        + jnp.maximum(jnp.maximum(moduli[0, 0], moduli[0, 1]), jnp.maximum(moduli[0, 2], moduli[0, 3]))
    )
    mu0 = 0.5 * (
        jnp.minimum(jnp.minimum(moduli[1, 0], moduli[1, 1]), jnp.minimum(moduli[1, 2], moduli[1, 3]))
        + jnp.maximum(jnp.maximum(moduli[1, 0], moduli[1, 1]), jnp.maximum(moduli[1, 2], moduli[1, 3]))
    )

    for load in loads:
        load.wait()
    lane = lax.broadcasted_iota(jnp.int32, (16, 128), 1)

    def emit(comp, mode, real, imag):
        first = jnp.where(lane < 64, real, pltpu.roll(imag, 64, 1))
        second = jnp.where(lane < 64, pltpu.roll(real, 64, 1), imag)
        unit = 4 * comp + 2 * mode
        send1[16 * unit : 16 * unit + 16, :] = first.astype(BF16)
        send1[16 * unit + 16 : 16 * unit + 32, :] = second.astype(BF16)

    def add(total, term):
        return term if total is None else total + term

    level_lam = [moduli[0, phase] for phase in range(NPHASE)]
    level_mu = [moduli[1, phase] for phase in range(NPHASE)]
    shared = [[None, None] for _ in range(MODES)]
    sums = [[[None, None] for _ in range(MODES)] for _ in range(3)]
    for plane in range(XW):
        phases = labels[plane]
        shift_lam = contrast(phases, level_lam, lam0, 1.0)
        shift_mu = contrast(phases, level_mu, mu0, 2.0)
        shear[plane] = shift_mu
        parts = [strain[comp, plane].astype(F32) for comp in range(3)]
        trace = shift_lam * (parts[0] + parts[1] + parts[2])
        parts = [shift_mu * part for part in parts]
        for mode in range(MODES):
            for side, weight in enumerate(wave(mode, plane)):
                if weight == 0.0:
                    continue
                shared[mode][side] = add(shared[mode][side], weight * trace)
                for comp in range(3):
                    sums[comp][mode][side] = add(sums[comp][mode][side], weight * parts[comp])
    for comp in range(3):
        for mode in range(MODES):
            emit(comp, mode, sums[comp][mode][0] + shared[mode][0], sums[comp][mode][1] + shared[mode][1])
    sums = [[[None, None] for _ in range(MODES)] for _ in range(3)]
    for plane in range(XW):
        shift_mu = shear[plane]
        parts = [shift_mu * strain[3 + comp, plane].astype(F32) for comp in range(3)]
        for mode in range(MODES):
            for side, weight in enumerate(wave(mode, plane)):
                if weight == 0.0:
                    continue
                for comp in range(3):
                    sums[comp][mode][side] = add(sums[comp][mode][side], weight * parts[comp])
    for comp in range(3):
        for mode in range(MODES):
            emit(3 + comp, mode, sums[comp][mode][0], sums[comp][mode][1])

    greetings = jnp.where(works_y, UNITS_Y - 1, UNITS_Y) + jnp.where(works_z, UNITS_Z - 1, UNITS_Z)
    pl.semaphore_wait(barrier, greetings)

    def tile(index, rows=16):
        return pl.ds(pl.multiple_of(index * rows, rows), rows)

    base = place_unit(pencil - jnp.where(works_y, 0, 3))

    def send_first(step):
        unit = lax.rem(base + step, UNITS_Y)
        pltpu.make_async_remote_copy(
            src_ref=send1.at[tile(unit)],
            dst_ref=land1.at[tile(pencil)],
            send_sem=send_sems.at[0],
            recv_sem=land_sems.at[0],
            device_id=(unit_place(unit), slab),
            device_id_type=MESH,
        ).start()

    @pl.when(works_y)
    def _():
        pltpu.make_async_copy(send1.at[tile(base)], land1.at[tile(pencil)], land_sems.at[0]).start()

    @pl.when(jnp.logical_not(works_y))
    def _():
        send_first(0)

    for step in range(1, UNITS_Y):
        send_first(step)

    for load in table_loads[:2]:
        load.wait()
    sin_y, cos_y = freq_y[0], freq_y[1]
    sin_z, cos_z = (jnp.tile(freq_z[i], (4, 1)) for i in range(2))
    cos_yz, sin_cos, cos_sin = cos_y * cos_z, sin_y * cos_z, cos_y * sin_z

    def exchange_2(step, own):
        owner = lax.rem(pencil + step, PENCIL)
        unit = place_unit(pencil)
        mine = unit_place(unit // 2)
        source = send2.at[tile(owner)]
        target = land2.at[tile(2 * slab + unit % 2)]
        if own:
            pltpu.make_async_copy(source, target, land_sems.at[1]).start()
        else:
            pltpu.make_async_remote_copy(
                src_ref=source,
                dst_ref=target,
                send_sem=send_sems.at[1],
                recv_sem=land_sems.at[1],
                device_id=(owner, mine),
                device_id_type=MESH,
            ).start()

    stays = unit_place(place_unit(pencil) // 2) == slab

    @pl.when(works_y)
    def _():
        table_loads[2].wait()
        pltpu.make_async_copy(land1, land1, land_sems.at[0]).wait()
        band = jnp.dot(along_y[...], with_swapped(land1[...]), preferred_element_type=F32)
        send2[...] = (band * (1 / math.sqrt(NY))).astype(BF16)

        @pl.when(stays)
        def _():
            exchange_2(0, True)

        @pl.when(jnp.logical_not(stays))
        def _():
            exchange_2(0, False)

        for step in range(1, PENCIL):
            exchange_2(step, False)

    for load in table_loads[3:]:
        load.wait()

    @pl.when(jnp.logical_not(works_y))
    def _():
        table_loads[2].wait()

    @pl.when(works_z)
    def _():
        unit = place_unit(slab)
        pltpu.make_async_copy(land2, land2, land_sems.at[1]).wait()
        band = transform_z(land2[...], coarse[...], turn, fine)
        for owner in range(SLAB):
            for half in range(2):
                pair = [band[8 * owner : 8 * owner + 8, 128 * q : 128 * q + 128] for q in (2 * half, 2 * half + 1)]
                start = 32 * owner + 16 * half
                send3[start : start + 16, :] = jnp.concatenate(pair, 0).astype(BF16)
        pltpu.make_async_copy(send3.at[tile(slab, 32)], land3.at[tile(unit, 32)], land_sems.at[2]).start()
        for step in range(1, SLAB):
            owner = lax.rem(slab + step, SLAB)
            pltpu.make_async_remote_copy(
                src_ref=send3.at[tile(owner, 32)],
                dst_ref=land3.at[tile(unit, 32)],
                send_sem=send_sems.at[2],
                recv_sem=land_sems.at[2],
                device_id=(pencil, owner),
                device_id_type=MESH,
            ).start()

    factor = (lam0 + mu0) / (mu0 * (lam0 + 2.0 * mu0))
    half_mu = 1.0 / (2.0 * mu0)
    pltpu.make_async_copy(land3, land3, land_sems.at[2]).wait()
    for mode in range(MODES):
        angle = math.pi / NX * (KX0 + mode)
        sin_x, cos_x = math.sin(angle), math.cos(angle)
        qx, qy, qz = sin_x * cos_yz, cos_x * sin_cos, cos_x * cos_sin
        inverse = 1.0 / jnp.maximum(qx * qx + qy * qy + qz * qz, Q_FLOOR)
        first = half_mu * inverse
        second = factor * inverse * inverse
        spectrum = []
        for comp in range(COMPS):
            start = 32 * (2 * comp + mode)
            spectrum.append(land3[start : start + 32, :].astype(F32))
        txx, tyy, tzz, tyz, txz, txy = spectrum
        vecx = txx * qx + txy * qy + txz * qz
        vecy = txy * qx + tyy * qy + tyz * qz
        vecz = txz * qx + tyz * qy + tzz * qz
        inner = second * (qx * vecx + qy * vecy + qz * vecz)
        vecx, vecy, vecz = first * vecx, first * vecy, first * vecz
        results = (
            qx * (inner * qx - 2.0 * vecx),
            qy * (inner * qy - 2.0 * vecy),
            qz * (inner * qz - 2.0 * vecz),
            inner * qy * qz - (qy * vecz + qz * vecy),
            inner * qx * qz - (qx * vecz + qz * vecx),
            inner * qx * qy - (qx * vecy + qy * vecx),
        )
        for comp, result in enumerate(results):
            for part in range(2):
                pieces = [result[8 * q + 4 * part : 8 * q + 4 * part + 4] for q in range(4)]
                out[comp, part, mode] = jnp.concatenate(pieces, 0)

    @pl.when(works_y)
    def _():
        gone = send1.at[pl.ds(0, 16 * (UNITS_Y - 1))]
        pltpu.make_async_copy(gone, gone, send_sems.at[0]).wait()

        @pl.when(stays)
        def _():
            gone = send2.at[pl.ds(0, 16 * (PENCIL - 1))]
            pltpu.make_async_copy(gone, gone, send_sems.at[1]).wait()

        @pl.when(jnp.logical_not(stays))
        def _():
            pltpu.make_async_copy(send2, send2, send_sems.at[1]).wait()

    @pl.when(jnp.logical_not(works_y))
    def _():
        pltpu.make_async_copy(send1, send1, send_sems.at[0]).wait()

    @pl.when(works_z)
    def _():
        gone = send3.at[pl.ds(0, 32 * (SLAB - 1))]
        pltpu.make_async_copy(gone, gone, send_sems.at[2]).wait()


def per_device(strain, labels, moduli):
    consts = tables()
    anywhere = pl.BlockSpec(memory_space=pl.ANY)
    return pl.pallas_call(
        kernel,
        out_shape=jax.ShapeDtypeStruct((COMPS, 2, MODES, 16, 128), F32),
        in_specs=[pl.BlockSpec(memory_space=pltpu.SMEM)] + [anywhere] * 8,
        out_specs=pl.BlockSpec(memory_space=pltpu.VMEM),
        scratch_shapes=[
            pltpu.VMEM((COMPS, XW, 16, 128), BF16),
            pltpu.VMEM((XW, 16, 128), jnp.int32),
            pltpu.VMEM((NY, 2 * NY), BF16),
            pltpu.VMEM((512, 1024), BF16),
            pltpu.VMEM((2, 32, 128), F32),
            pltpu.VMEM((4, 128, 128), BF16),
            pltpu.VMEM((2, 32, 128), F32),
            pltpu.VMEM((2, 8, 128), F32),
            pltpu.VMEM((XW, 16, 128), F32),
            pltpu.VMEM((16 * UNITS_Y, 128), BF16),
            pltpu.VMEM((16 * PENCIL, 128), BF16),
            pltpu.VMEM((16 * PENCIL, 128), BF16),
            pltpu.VMEM((32 * SLAB, 128), BF16),
            pltpu.VMEM((32 * SLAB, 128), BF16),
            pltpu.VMEM((32 * UNITS_Z, 128), BF16),
            pltpu.SemaphoreType.DMA((2,)),
            pltpu.SemaphoreType.DMA((6,)),
            pltpu.SemaphoreType.DMA((3,)),
            pltpu.SemaphoreType.DMA((3,)),
        ],
        compiler_params=pltpu.CompilerParams(
            collective_id=0, has_side_effects=True, vmem_limit_bytes=32 * 1024 * 1024
        ),
    )(moduli, strain, labels, *(jnp.asarray(const) for const in consts))


def solution(mesh):
    return jax.shard_map(
        per_device,
        mesh=mesh,
        in_specs=(P(None, None, "pencil", "slab"), P(None, "pencil", "slab"), P()),
        out_specs=P(None, None, None, "pencil", "slab"),
        check_vma=False,
    )
```

```python
import math

import jax
import jax.numpy as jnp
import numpy as np
from jax import lax
from jax.experimental import pallas as pl
from jax.experimental.pallas import tpu as pltpu
from jax.sharding import PartitionSpec as P

MESH = pl.DeviceIdType.MESH
NX, NY, NZ = 2048, 512, 2048
XW, MODES, KX0, NPHASE, COMPS = 16, 2, 64, 4, 6
PENCIL, SLAB = 32, 16
UNITS_Y, UNITS_Z = 24, 12
Q_FLOOR = 0.01
F32, BF16 = jnp.float32, jnp.bfloat16


def z_place(unit, owner):
    return lax.rem(unit + owner, UNITS_Z)


def z_unit(place, owner):
    return lax.rem(place + 3 * UNITS_Z - owner, UNITS_Z)


def far_first(chips, each):
    order = sorted(range(chips), key=lambda step: -min(step, chips - step))
    return [chip * each + i for chip in order for i in reversed(range(each))]


def tables():
    angle = 2 * math.pi / NY * (np.outer(np.arange(NY), np.arange(NY)) % NY)
    along_y = np.concatenate([np.cos(angle), np.sin(angle)], 1)
    angle = 2 * math.pi / 32 * (np.outer(np.arange(32), np.arange(32)) % 32)
    same = np.eye(16)
    coarse = [np.einsum("bt,kj->kbtj", f(angle), same).reshape(512, 512) for f in (np.cos, np.sin)]
    coarse = np.concatenate(coarse, 1)
    angle = 2 * math.pi / NZ * np.outer(np.arange(32), np.arange(64))
    scale = 1 / math.sqrt(NZ)
    turn = np.stack([np.tile(np.cos(angle), 2), np.concatenate([np.sin(angle), -np.sin(angle)], 1)]) * scale
    angle = 2 * math.pi / 64 * (np.outer(np.arange(64), np.arange(64)) % 64)
    cosine, sine = np.cos(angle), np.sin(angle)
    fine = np.stack([np.concatenate([cosine, sine], 1), np.concatenate([-sine, cosine], 1)])
    fine = fine.reshape(2, 16, 4, 128).transpose(1, 0, 2, 3)
    fine = np.stack([np.roll(fine, -delta, 2).reshape(128, 128) for delta in range(4)])
    rows = np.arange(32)
    ky = 16 * np.arange(PENCIL)[:, None] + (rows // 8 * 4 + rows % 4)[None, :]
    angle = np.broadcast_to((math.pi / NY * ky)[:, :, None], (PENCIL, 32, 128))
    freq_y = np.stack([np.sin(angle), np.cos(angle)], 1)
    angle = math.pi / NZ * np.arange(NZ).reshape(SLAB, 1, 128)
    angle = np.broadcast_to(angle, (SLAB, 8, 128))
    freq_z = np.stack([np.sin(angle), np.cos(angle)], 1)
    return (
        along_y.astype(BF16),
        coarse.astype(BF16),
        turn.astype(np.float32),
        fine.astype(BF16),
        freq_y.astype(np.float32),
        freq_z.astype(np.float32),
    )


def swap_parts(values):
    lane = lax.broadcasted_iota(jnp.int32, values.shape, 1)
    turned = pltpu.roll(values, 64, 1)
    return jnp.where(lane < 64, turned, -turned)


def with_swapped(tile):
    return jnp.concatenate([tile, swap_parts(tile.astype(F32)).astype(BF16)], 0)


def transform_z(data, coarse, turn, fine):
    mixed = jnp.dot(coarse, with_swapped(data), preferred_element_type=F32)
    swapped = pltpu.roll(mixed, 64, 1)
    mixed = mixed.reshape(16, 32, 128) * turn[0][None] + swapped.reshape(16, 32, 128) * turn[1][None]
    mixed = mixed.reshape(512, 128).astype(BF16)
    blocks = [mixed[32 * k : 32 * k + 32] for k in range(16)]
    row = lax.broadcasted_iota(jnp.int32, (128, 512), 0)
    lane = lax.broadcasted_iota(jnp.int32, (128, 512), 1)
    shift = (lane // 32 - row) & 3
    result = None
    for delta in range(4):
        turned = jnp.concatenate([blocks[4 * (k // 4) + (k - delta) % 4] for k in range(16)], 0)
        part = lax.dot_general(fine[delta], turned, (((1,), (1,)), ((), ())), preferred_element_type=F32)
        result = part if result is None else jnp.where(shift == delta, part, result)
    return result


def contrast(labels, values, base, factor):
    levels = [(values[phase] - base) * factor for phase in range(NPHASE)]
    chosen = jnp.where(labels == 2, levels[2], levels[3])
    chosen = jnp.where(labels == 1, levels[1], chosen)
    return jnp.where(labels == 0, levels[0], chosen)


def wave(mode, plane):
    angle = 2 * math.pi / NX * ((KX0 + mode) * plane % NX)
    scale = 1 / math.sqrt(XW)
    return float(math.cos(angle) * scale), float(-math.sin(angle) * scale)


def kernel(
    moduli_hbm,
    strain_hbm,
    labels_hbm,
    along_y_hbm,
    coarse_hbm,
    turn_hbm,
    fine_hbm,
    freq_y_hbm,
    freq_z_hbm,
    out,
    moduli,
    strain,
    labels,
    along_y,
    coarse,
    turn,
    fine,
    freq_y,
    freq_z,
    shear,
    send1,
    land1,
    send2,
    land2,
    send3,
    land3,
    in_sems,
    table_sems,
    send_sems,
    land_sems,
):
    pencil = lax.axis_index("pencil")
    slab = lax.axis_index("slab")
    works_y = pencil < UNITS_Y
    works_z = slab < UNITS_Z

    moduli_load = pltpu.make_async_copy(moduli_hbm, moduli, in_sems.at[2])
    moduli_load.start()
    loads = [
        pltpu.make_async_copy(strain_hbm, strain, in_sems.at[0]),
        pltpu.make_async_copy(labels_hbm, labels, in_sems.at[1]),
    ]
    for load in loads:
        load.start()
    pairs = [
        (freq_y_hbm.at[pencil], freq_y),
        (freq_z_hbm.at[slab], freq_z),
        (along_y_hbm, along_y),
        (coarse_hbm, coarse),
        (turn_hbm, turn),
        (fine_hbm, fine),
    ]
    table_loads = [pltpu.make_async_copy(a, b, table_sems.at[i]) for i, (a, b) in enumerate(pairs)]
    for load in table_loads:
        load.start()

    barrier = pltpu.get_barrier_semaphore()

    @pl.when(works_y)
    def _():
        for step in far_first(8, 4)[:-1]:
            other = lax.rem(pencil + step, PENCIL)
            pl.semaphore_signal(barrier, inc=1, device_id=(other, slab), device_id_type=MESH)

    @pl.when(works_z)
    def _():
        for step in far_first(8, 2)[:-1]:
            other = lax.rem(slab + step, SLAB)
            pl.semaphore_signal(barrier, inc=1, device_id=(pencil, other), device_id_type=MESH)

    moduli_load.wait()
    lam0 = 0.5 * (
        jnp.minimum(jnp.minimum(moduli[0, 0], moduli[0, 1]), jnp.minimum(moduli[0, 2], moduli[0, 3]))
        + jnp.maximum(jnp.maximum(moduli[0, 0], moduli[0, 1]), jnp.maximum(moduli[0, 2], moduli[0, 3]))
    )
    mu0 = 0.5 * (
        jnp.minimum(jnp.minimum(moduli[1, 0], moduli[1, 1]), jnp.minimum(moduli[1, 2], moduli[1, 3]))
        + jnp.maximum(jnp.maximum(moduli[1, 0], moduli[1, 1]), jnp.maximum(moduli[1, 2], moduli[1, 3]))
    )

    for load in loads:
        load.wait()
    lane = lax.broadcasted_iota(jnp.int32, (16, 128), 1)

    def emit(comp, mode, real, imag):
        first = jnp.where(lane < 64, real, pltpu.roll(imag, 64, 1))
        second = jnp.where(lane < 64, pltpu.roll(real, 64, 1), imag)
        unit = 4 * comp + 2 * mode
        send1[16 * unit : 16 * unit + 16, :] = first.astype(BF16)
        send1[16 * unit + 16 : 16 * unit + 32, :] = second.astype(BF16)

    def add(total, term):
        return term if total is None else total + term

    level_lam = [moduli[0, phase] for phase in range(NPHASE)]
    level_mu = [moduli[1, phase] for phase in range(NPHASE)]
    shared = [[None, None] for _ in range(MODES)]
    sums = [[[None, None] for _ in range(MODES)] for _ in range(3)]
    for plane in range(XW):
        phases = labels[plane]
        shift_lam = contrast(phases, level_lam, lam0, 1.0)
        shift_mu = contrast(phases, level_mu, mu0, 2.0)
        shear[plane] = shift_mu
        parts = [strain[comp, plane].astype(F32) for comp in range(3)]
        trace = shift_lam * (parts[0] + parts[1] + parts[2])
        parts = [shift_mu * part for part in parts]
        for mode in range(MODES):
            for side, weight in enumerate(wave(mode, plane)):
                if weight == 0.0:
                    continue
                shared[mode][side] = add(shared[mode][side], weight * trace)
                for comp in range(3):
                    sums[comp][mode][side] = add(sums[comp][mode][side], weight * parts[comp])
    for comp in range(3):
        for mode in range(MODES):
            emit(comp, mode, sums[comp][mode][0] + shared[mode][0], sums[comp][mode][1] + shared[mode][1])
    sums = [[[None, None] for _ in range(MODES)] for _ in range(3)]
    for plane in range(XW):
        shift_mu = shear[plane]
        parts = [shift_mu * strain[3 + comp, plane].astype(F32) for comp in range(3)]
        for mode in range(MODES):
            for side, weight in enumerate(wave(mode, plane)):
                if weight == 0.0:
                    continue
                for comp in range(3):
                    sums[comp][mode][side] = add(sums[comp][mode][side], weight * parts[comp])
    for comp in range(3):
        for mode in range(MODES):
            emit(3 + comp, mode, sums[comp][mode][0], sums[comp][mode][1])

    greetings = jnp.where(works_y, UNITS_Y - 1, UNITS_Y) + jnp.where(works_z, UNITS_Z - 1, UNITS_Z)
    pl.semaphore_wait(barrier, greetings)

    def tile(index, rows=16):
        return pl.ds(pl.multiple_of(index * rows, rows), rows)

    def send_first(unit):
        pltpu.make_async_remote_copy(
            src_ref=send1.at[tile(unit)],
            dst_ref=land1.at[tile(pencil)],
            send_sem=send_sems.at[0],
            recv_sem=land_sems.at[0],
            device_id=(unit, slab),
            device_id_type=MESH,
        ).start()

    for step in far_first(8, 4)[:-1]:
        unit = lax.rem(pencil + step, PENCIL)

        @pl.when(unit < UNITS_Y)
        def _():
            send_first(unit)

    @pl.when(works_y)
    def _():
        pltpu.make_async_copy(send1.at[tile(pencil)], land1.at[tile(pencil)], land_sems.at[0]).start()

    for load in table_loads[:2]:
        load.wait()
    sin_y, cos_y = freq_y[0], freq_y[1]
    sin_z, cos_z = (jnp.tile(freq_z[i], (4, 1)) for i in range(2))
    cos_yz, sin_cos, cos_sin = cos_y * cos_z, sin_y * cos_z, cos_y * sin_z

    def exchange_2(step, own):
        owner = lax.rem(pencil + step, PENCIL)
        mine = z_place(pencil // 2, owner)
        source = send2.at[tile(owner)]
        target = land2.at[tile(2 * slab + pencil % 2)]
        if own:
            pltpu.make_async_copy(source, target, land_sems.at[1]).start()
        else:
            pltpu.make_async_remote_copy(
                src_ref=source,
                dst_ref=target,
                send_sem=send_sems.at[1],
                recv_sem=land_sems.at[1],
                device_id=(owner, mine),
                device_id_type=MESH,
            ).start()

    stays = z_place(pencil // 2, pencil) == slab

    @pl.when(works_y)
    def _():
        table_loads[2].wait()
        pltpu.make_async_copy(land1, land1, land_sems.at[0]).wait()
        band = jnp.dot(along_y[...], with_swapped(land1[...]), preferred_element_type=F32)
        send2[...] = (band * (1 / math.sqrt(NY))).astype(BF16)

        for step in far_first(8, 4)[:-1]:
            exchange_2(step, False)

        @pl.when(stays)
        def _():
            exchange_2(0, True)

        @pl.when(jnp.logical_not(stays))
        def _():
            exchange_2(0, False)

    for load in table_loads[3:]:
        load.wait()

    @pl.when(jnp.logical_not(works_y))
    def _():
        table_loads[2].wait()

    @pl.when(works_z)
    def _():
        unit = z_unit(slab, pencil)
        pltpu.make_async_copy(land2, land2, land_sems.at[1]).wait()
        band = transform_z(land2[...], coarse[...], turn, fine)
        for owner in range(SLAB):
            for half in range(2):
                pair = [band[8 * owner : 8 * owner + 8, 128 * q : 128 * q + 128] for q in (2 * half, 2 * half + 1)]
                start = 32 * owner + 16 * half
                send3[start : start + 16, :] = jnp.concatenate(pair, 0).astype(BF16)
        for step in far_first(8, 2)[:-1]:
            owner = lax.rem(slab + step, SLAB)
            pltpu.make_async_remote_copy(
                src_ref=send3.at[tile(owner, 32)],
                dst_ref=land3.at[tile(unit, 32)],
                send_sem=send_sems.at[2],
                recv_sem=land_sems.at[2],
                device_id=(pencil, owner),
                device_id_type=MESH,
            ).start()
        pltpu.make_async_copy(send3.at[tile(slab, 32)], land3.at[tile(unit, 32)], land_sems.at[2]).start()

    factor = (lam0 + mu0) / (mu0 * (lam0 + 2.0 * mu0))
    half_mu = 1.0 / (2.0 * mu0)
    pltpu.make_async_copy(land3, land3, land_sems.at[2]).wait()
    for mode in range(MODES):
        angle = math.pi / NX * (KX0 + mode)
        sin_x, cos_x = math.sin(angle), math.cos(angle)
        qx, qy, qz = sin_x * cos_yz, cos_x * sin_cos, cos_x * cos_sin
        inverse = 1.0 / jnp.maximum(qx * qx + qy * qy + qz * qz, Q_FLOOR)
        first = half_mu * inverse
        second = factor * inverse * inverse
        spectrum = []
        for comp in range(COMPS):
            start = 32 * (2 * comp + mode)
            spectrum.append(land3[start : start + 32, :].astype(F32))
        txx, tyy, tzz, tyz, txz, txy = spectrum
        vecx = txx * qx + txy * qy + txz * qz
        vecy = txy * qx + tyy * qy + tyz * qz
        vecz = txz * qx + tyz * qy + tzz * qz
        inner = second * (qx * vecx + qy * vecy + qz * vecz)
        vecx, vecy, vecz = first * vecx, first * vecy, first * vecz
        results = (
            qx * (inner * qx - 2.0 * vecx),
            qy * (inner * qy - 2.0 * vecy),
            qz * (inner * qz - 2.0 * vecz),
            inner * qy * qz - (qy * vecz + qz * vecy),
            inner * qx * qz - (qx * vecz + qz * vecx),
            inner * qx * qy - (qx * vecy + qy * vecx),
        )
        for comp, result in enumerate(results):
            for part in range(2):
                pieces = [result[8 * q + 4 * part : 8 * q + 4 * part + 4] for q in range(4)]
                out[comp, part, mode] = jnp.concatenate(pieces, 0)

    @pl.when(works_y)
    def _():
        gone = send1.at[pl.ds(0, 16 * (UNITS_Y - 1))]
        pltpu.make_async_copy(gone, gone, send_sems.at[0]).wait()

        @pl.when(stays)
        def _():
            gone = send2.at[pl.ds(0, 16 * (PENCIL - 1))]
            pltpu.make_async_copy(gone, gone, send_sems.at[1]).wait()

        @pl.when(jnp.logical_not(stays))
        def _():
            pltpu.make_async_copy(send2, send2, send_sems.at[1]).wait()

    @pl.when(jnp.logical_not(works_y))
    def _():
        pltpu.make_async_copy(send1, send1, send_sems.at[0]).wait()

    @pl.when(works_z)
    def _():
        gone = send3.at[pl.ds(0, 32 * (SLAB - 1))]
        pltpu.make_async_copy(gone, gone, send_sems.at[2]).wait()


def per_device(strain, labels, moduli):
    consts = [jnp.asarray(const) for const in tables()]
    moduli, strain, labels, *consts = [
        pltpu.with_memory_space_constraint(x, pltpu.HBM) for x in (moduli, strain, labels, *consts)
    ]
    anywhere = pl.BlockSpec(memory_space=pltpu.HBM)
    return pl.pallas_call(
        kernel,
        out_shape=jax.ShapeDtypeStruct((COMPS, 2, MODES, 16, 128), F32),
        in_specs=[anywhere] * 9,
        out_specs=pl.BlockSpec(memory_space=pltpu.VMEM),
        scratch_shapes=[
            pltpu.SMEM((2, NPHASE), F32),
            pltpu.VMEM((COMPS, XW, 16, 128), BF16),
            pltpu.VMEM((XW, 16, 128), jnp.int32),
            pltpu.VMEM((NY, 2 * NY), BF16),
            pltpu.VMEM((512, 1024), BF16),
            pltpu.VMEM((2, 32, 128), F32),
            pltpu.VMEM((4, 128, 128), BF16),
            pltpu.VMEM((2, 32, 128), F32),
            pltpu.VMEM((2, 8, 128), F32),
            pltpu.VMEM((XW, 16, 128), F32),
            pltpu.VMEM((16 * UNITS_Y, 128), BF16),
            pltpu.VMEM((16 * PENCIL, 128), BF16),
            pltpu.VMEM((16 * PENCIL, 128), BF16),
            pltpu.VMEM((32 * SLAB, 128), BF16),
            pltpu.VMEM((32 * SLAB, 128), BF16),
            pltpu.VMEM((32 * UNITS_Z, 128), BF16),
            pltpu.SemaphoreType.DMA((3,)),
            pltpu.SemaphoreType.DMA((6,)),
            pltpu.SemaphoreType.DMA((3,)),
            pltpu.SemaphoreType.DMA((3,)),
        ],
        compiler_params=pltpu.CompilerParams(
            collective_id=0, has_side_effects=True, vmem_limit_bytes=32 * 1024 * 1024
        ),
    )(moduli, strain, labels, *consts)


def solution(mesh):
    return jax.shard_map(
        per_device,
        mesh=mesh,
        in_specs=(P(None, None, "pencil", "slab"), P(None, "pencil", "slab"), P()),
        out_specs=P(None, None, None, "pencil", "slab"),
        check_vma=False,
    )
```

```python
import math

import jax
import jax.numpy as jnp
import numpy as np
from jax import lax
from jax.experimental import pallas as pl
from jax.experimental.pallas import tpu as pltpu
from jax.sharding import PartitionSpec as P

MESH = pl.DeviceIdType.MESH
NX, NY, NZ = 2048, 512, 2048
XW, MODES, KX0, NPHASE, COMPS = 16, 2, 64, 4, 6
PENCIL, SLAB = 32, 16
UNITS = 12
SLAB_ORDER = (0, 1, 2, 3, 14, 15, 4, 5, 12, 13, 6, 7, 10, 11, 8, 9)
Q_FLOOR = 0.01
F32, BF16 = jnp.float32, jnp.bfloat16


def z_place(unit, owner):
    return lax.rem(lax.rem(unit + owner, UNITS) + SLAB - 4, SLAB)


def z_unit(place, owner):
    return lax.rem(lax.rem(place + 4, SLAB) + 3 * UNITS - owner, UNITS)


def far_first(chips, each):
    order = sorted(range(chips), key=lambda step: -min(step, chips - step))
    return [chip * each + i for chip in order for i in reversed(range(each))]


def parts_table(angle):
    cosine, sine = np.cos(angle), np.sin(angle)
    return np.stack([np.stack([cosine, sine], 1), np.stack([-sine, cosine], 1)])


def tables():
    angle = 2 * math.pi / NY * (np.outer(np.arange(NY), np.arange(NY)) % NY)
    along_y = parts_table(angle).reshape(2, PENCIL, 16, 2, PENCIL, 16)
    along_y = along_y.transpose(1, 0, 2, 4, 3, 5).reshape(2 * NY, 2 * NY)
    angle = 2 * math.pi / 16 * (np.outer(np.arange(16), np.arange(16)) % 16)
    coarse = np.einsum("obrs,kj->okbsrj", parts_table(angle), np.eye(16)).reshape(512, 512)
    angle = 2 * math.pi / NZ * np.outer(np.arange(16), np.arange(128))
    turn = np.stack([np.cos(angle), np.sin(angle)]) / math.sqrt(NZ)
    angle = 2 * math.pi / 128 * (np.outer(np.arange(128), np.arange(128)) % 128)
    fine = parts_table(angle).reshape(2, SLAB, 8, 256)[:, list(SLAB_ORDER)].transpose(1, 0, 2, 3)
    fine = np.stack([np.roll(fine, -delta, 2).reshape(256, 256) for delta in range(8)])
    angle = math.pi / NY * np.arange(NY).reshape(PENCIL, 16, 1)
    angle = np.broadcast_to(angle, (PENCIL, 16, 128))
    freq_y = np.stack([np.sin(angle), np.cos(angle)], 1)
    angle = math.pi / NZ * np.arange(NZ).reshape(SLAB, 1, 128)
    angle = np.broadcast_to(angle, (SLAB, 8, 128))
    freq_z = np.stack([np.sin(angle), np.cos(angle)], 1)
    return (
        along_y.astype(BF16),
        coarse.astype(BF16),
        turn.astype(np.float32),
        fine.astype(BF16),
        freq_y.astype(np.float32),
        freq_z.astype(np.float32),
    )


def transform_z(data, coarse, turn):
    mixed = jnp.dot(coarse, data, preferred_element_type=F32).reshape(2, 16, 16, 128)
    cosine, sine = turn[0][None], turn[1][None]
    real = mixed[0] * cosine + mixed[1] * sine
    imag = mixed[1] * cosine - mixed[0] * sine
    parts = [part.reshape(256, 128).astype(BF16) for part in (real, imag)]
    return jnp.concatenate(parts, 1)


def last_points(turned, fine, start, size):
    row = lax.broadcasted_iota(jnp.int32, (size, 256), 0)
    lane = lax.broadcasted_iota(jnp.int32, (size, 256), 1)
    shift = (lane // 16 - row) & 7
    result = None
    for delta in range(8):
        part = lax.dot_general(
            fine[delta, start : start + size, :], turned[delta], (((1,), (1,)), ((), ())), preferred_element_type=F32
        )
        result = part if result is None else jnp.where(shift == delta, part, result)
    return result


def contrast(labels, values, base, factor):
    levels = [(values[phase] - base) * factor for phase in range(NPHASE)]
    chosen = jnp.where(labels == 2, levels[2], levels[3])
    chosen = jnp.where(labels == 1, levels[1], chosen)
    return jnp.where(labels == 0, levels[0], chosen)


def wave(mode, plane):
    angle = 2 * math.pi / NX * ((KX0 + mode) * plane % NX)
    scale = 1 / math.sqrt(XW)
    return float(math.cos(angle) * scale), float(-math.sin(angle) * scale)


def kernel(
    moduli_hbm,
    strain_hbm,
    labels_hbm,
    along_y_hbm,
    coarse_hbm,
    turn_hbm,
    fine_hbm,
    freq_y_hbm,
    freq_z_hbm,
    out,
    moduli,
    strain,
    labels,
    along_y,
    coarse,
    turn,
    fine,
    freq_y,
    freq_z,
    shear,
    send1,
    land1,
    send2,
    land2,
    send3,
    land3,
    in_sems,
    table_sems,
    send_sems,
    land_sems,
):
    pencil = lax.axis_index("pencil")
    slab = lax.axis_index("slab")
    works_y = (pencil < 24) & (pencil % 2 == 0)
    unit_y = pencil // 4 * 2 + pencil % 4 // 2
    works_z = lax.rem(slab + 4, SLAB) < UNITS

    barrier = pltpu.get_barrier_semaphore()

    @pl.when(works_y)
    def _():
        for step in far_first(8, 4)[:-1]:
            other = lax.rem(pencil + step, PENCIL)
            pl.semaphore_signal(barrier, inc=1, device_id=(other, slab), device_id_type=MESH)

    @pl.when(works_z)
    def _():
        for step in far_first(8, 2)[:-1]:
            other = lax.rem(slab + step, SLAB)
            pl.semaphore_signal(barrier, inc=1, device_id=(pencil, other), device_id_type=MESH)

    moduli_load = pltpu.make_async_copy(moduli_hbm, moduli, in_sems.at[2])
    moduli_load.start()
    loads = [
        pltpu.make_async_copy(strain_hbm, strain, in_sems.at[0]),
        pltpu.make_async_copy(labels_hbm, labels, in_sems.at[1]),
    ]
    for load in loads:
        load.start()
    pairs = [
        (freq_y_hbm.at[pencil], freq_y),
        (freq_z_hbm.at[slab], freq_z),
        (along_y_hbm, along_y),
        (coarse_hbm, coarse),
        (turn_hbm, turn),
        (fine_hbm, fine),
    ]
    table_loads = [pltpu.make_async_copy(a, b, table_sems.at[i]) for i, (a, b) in enumerate(pairs)]
    for load in table_loads:
        load.start()

    moduli_load.wait()
    lam0 = 0.5 * (
        jnp.minimum(jnp.minimum(moduli[0, 0], moduli[0, 1]), jnp.minimum(moduli[0, 2], moduli[0, 3]))
        + jnp.maximum(jnp.maximum(moduli[0, 0], moduli[0, 1]), jnp.maximum(moduli[0, 2], moduli[0, 3]))
    )
    mu0 = 0.5 * (
        jnp.minimum(jnp.minimum(moduli[1, 0], moduli[1, 1]), jnp.minimum(moduli[1, 2], moduli[1, 3]))
        + jnp.maximum(jnp.maximum(moduli[1, 0], moduli[1, 1]), jnp.maximum(moduli[1, 2], moduli[1, 3]))
    )

    for load in loads:
        load.wait()

    def emit(comp, mode, real, imag):
        start = 32 * (2 * comp + mode)
        send1[start : start + 16, :] = real.astype(BF16)
        send1[start + 16 : start + 32, :] = imag.astype(BF16)

    def add(total, term):
        return term if total is None else total + term

    level_lam = [moduli[0, phase] for phase in range(NPHASE)]
    level_mu = [moduli[1, phase] for phase in range(NPHASE)]
    shared = [[None, None] for _ in range(MODES)]
    sums = [[[None, None] for _ in range(MODES)] for _ in range(3)]
    for plane in range(XW):
        phases = labels[plane]
        shift_lam = contrast(phases, level_lam, lam0, 1.0)
        shift_mu = contrast(phases, level_mu, mu0, 2.0)
        shear[plane] = shift_mu
        parts = [strain[comp, plane].astype(F32) for comp in range(3)]
        trace = shift_lam * (parts[0] + parts[1] + parts[2])
        parts = [shift_mu * part for part in parts]
        for mode in range(MODES):
            for side, weight in enumerate(wave(mode, plane)):
                if weight == 0.0:
                    continue
                shared[mode][side] = add(shared[mode][side], weight * trace)
                for comp in range(3):
                    sums[comp][mode][side] = add(sums[comp][mode][side], weight * parts[comp])
    for comp in range(3):
        for mode in range(MODES):
            emit(comp, mode, sums[comp][mode][0] + shared[mode][0], sums[comp][mode][1] + shared[mode][1])
    sums = [[[None, None] for _ in range(MODES)] for _ in range(3)]
    for plane in range(XW):
        shift_mu = shear[plane]
        parts = [shift_mu * strain[3 + comp, plane].astype(F32) for comp in range(3)]
        for mode in range(MODES):
            for side, weight in enumerate(wave(mode, plane)):
                if weight == 0.0:
                    continue
                for comp in range(3):
                    sums[comp][mode][side] = add(sums[comp][mode][side], weight * parts[comp])
    for comp in range(3):
        for mode in range(MODES):
            emit(3 + comp, mode, sums[comp][mode][0], sums[comp][mode][1])

    greetings = jnp.where(works_y, UNITS - 1, UNITS) + jnp.where(works_z, UNITS - 1, UNITS)
    pl.semaphore_wait(barrier, greetings)

    def tile(index):
        return pl.ds(pl.multiple_of(index * 32, 32), 32)

    for unit in (10, 11, 8, 9, 6, 7, 4, 5, 2, 3, 0, 1):
        place = 4 * (unit // 2) + 2 * (unit % 2)

        @pl.when(pencil != place)
        def _():
            pltpu.make_async_remote_copy(
                src_ref=send1.at[tile(unit)],
                dst_ref=land1.at[tile(pencil)],
                send_sem=send_sems.at[0],
                recv_sem=land_sems.at[0],
                device_id=(place, slab),
                device_id_type=MESH,
            ).start()

    @pl.when(works_y)
    def _():
        pltpu.make_async_copy(send1.at[tile(unit_y)], land1.at[tile(pencil)], land_sems.at[0]).start()

    for load in table_loads[:2]:
        load.wait()
    sin_y, cos_y = freq_y[0], freq_y[1]
    sin_z, cos_z = (jnp.tile(freq_z[i], (2, 1)) for i in range(2))
    cos_yz, sin_cos, cos_sin = cos_y * cos_z, sin_y * cos_z, cos_y * sin_z

    def exchange_2(owner, own):
        mine = z_place(unit_y, owner)
        source = send2.at[tile(owner)]
        target = land2.at[tile(slab)]
        if own:
            pltpu.make_async_copy(source, target, land_sems.at[1]).start()
        else:
            pltpu.make_async_remote_copy(
                src_ref=source,
                dst_ref=target,
                send_sem=send_sems.at[1],
                recv_sem=land_sems.at[1],
                device_id=(owner, mine),
                device_id_type=MESH,
            ).start()

    stays = z_place(unit_y, pencil) == slab

    @pl.when(works_y)
    def _():
        table_loads[2].wait()
        pltpu.make_async_copy(land1, land1, land_sems.at[0]).wait()
        for chunk in range(4):
            rows = slice(256 * chunk, 256 * chunk + 256)
            band = jnp.dot(along_y[rows, :], land1[...], preferred_element_type=F32)
            send2[rows, :] = (band * (1 / math.sqrt(NY))).astype(BF16)
            for owner in range(8 * chunk, 8 * chunk + 8):
                own = stays & (pencil == owner)

                @pl.when(own)
                def _():
                    exchange_2(owner, True)

                @pl.when(jnp.logical_not(own))
                def _():
                    exchange_2(owner, False)

    for load in table_loads[3:]:
        load.wait()

    @pl.when(jnp.logical_not(works_y))
    def _():
        table_loads[2].wait()

    @pl.when(works_z)
    def _():
        unit = z_unit(slab, pencil)
        pltpu.make_async_copy(land2, land2, land_sems.at[1]).wait()
        band = transform_z(land2[...], coarse[...], turn)
        blocks = [band[16 * k : 16 * k + 16] for k in range(16)]
        turned = [
            jnp.concatenate([blocks[8 * (k // 8) + (k - delta) % 8] for k in range(16)], 0) for delta in range(8)
        ]
        for chunk in range(2):
            points = last_points(turned, fine, 128 * chunk, 128)
            for place, owner in enumerate(SLAB_ORDER[8 * chunk : 8 * chunk + 8]):
                for part in range(2):
                    row, start = 16 * place + 8 * part, 32 * owner + 16 * part
                    halves = [points[row : row + 8, 128 * half : 128 * half + 128] for half in range(2)]
                    send3[start : start + 16, :] = jnp.concatenate(halves, 0).astype(BF16)
            for owner in SLAB_ORDER[8 * chunk : 8 * chunk + 8]:
                source, target = send3.at[tile(owner)], land3.at[tile(unit)]

                @pl.when(slab == owner)
                def _():
                    pltpu.make_async_copy(source, target, land_sems.at[2]).start()

                @pl.when(slab != owner)
                def _():
                    pltpu.make_async_remote_copy(
                        src_ref=source,
                        dst_ref=target,
                        send_sem=send_sems.at[2],
                        recv_sem=land_sems.at[2],
                        device_id=(pencil, owner),
                        device_id_type=MESH,
                    ).start()

    factor = (lam0 + mu0) / (mu0 * (lam0 + 2.0 * mu0))
    half_mu = 1.0 / (2.0 * mu0)
    weights = []
    for mode in range(MODES):
        angle = math.pi / NX * (KX0 + mode)
        sin_x, cos_x = math.sin(angle), math.cos(angle)
        qx, qy, qz = sin_x * cos_yz, cos_x * sin_cos, cos_x * cos_sin
        inverse = 1.0 / jnp.maximum(qx * qx + qy * qy + qz * qz, Q_FLOOR)
        weights.append((qx, qy, qz, half_mu * inverse, factor * inverse * inverse))
    pltpu.make_async_copy(land3, land3, land_sems.at[2]).wait()
    for mode in range(MODES):
        qx, qy, qz, first, second = weights[mode]
        for part in range(2):
            spectrum = []
            for comp in range(COMPS):
                start = 32 * (2 * comp + mode) + 16 * part
                spectrum.append(land3[start : start + 16, :].astype(F32))
            txx, tyy, tzz, tyz, txz, txy = spectrum
            vecx = txx * qx + txy * qy + txz * qz
            vecy = txy * qx + tyy * qy + tyz * qz
            vecz = txz * qx + tyz * qy + tzz * qz
            inner = second * (qx * vecx + qy * vecy + qz * vecz)
            vecx, vecy, vecz = first * vecx, first * vecy, first * vecz
            out[0, part, mode] = qx * (inner * qx - 2.0 * vecx)
            out[1, part, mode] = qy * (inner * qy - 2.0 * vecy)
            out[2, part, mode] = qz * (inner * qz - 2.0 * vecz)
            out[3, part, mode] = inner * qy * qz - (qy * vecz + qz * vecy)
            out[4, part, mode] = inner * qx * qz - (qx * vecz + qz * vecx)
            out[5, part, mode] = inner * qx * qy - (qx * vecy + qy * vecx)

    @pl.when(works_y)
    def _():
        gone = send1.at[pl.ds(0, 32 * (UNITS - 1))]
        pltpu.make_async_copy(gone, gone, send_sems.at[0]).wait()

        @pl.when(stays)
        def _():
            gone = send2.at[pl.ds(0, 32 * (PENCIL - 1))]
            pltpu.make_async_copy(gone, gone, send_sems.at[1]).wait()

        @pl.when(jnp.logical_not(stays))
        def _():
            pltpu.make_async_copy(send2, send2, send_sems.at[1]).wait()

    @pl.when(jnp.logical_not(works_y))
    def _():
        pltpu.make_async_copy(send1, send1, send_sems.at[0]).wait()

    @pl.when(works_z)
    def _():
        gone = send3.at[pl.ds(0, 32 * (SLAB - 1))]
        pltpu.make_async_copy(gone, gone, send_sems.at[2]).wait()


def per_device(strain, labels, moduli):
    consts = [jnp.asarray(const) for const in tables()]
    moduli, strain, labels, *consts = [
        pltpu.with_memory_space_constraint(x, pltpu.HBM) for x in (moduli, strain, labels, *consts)
    ]
    anywhere = pl.BlockSpec(memory_space=pltpu.HBM)
    return pl.pallas_call(
        kernel,
        out_shape=jax.ShapeDtypeStruct((COMPS, 2, MODES, 16, 128), F32),
        in_specs=[anywhere] * 9,
        out_specs=pl.BlockSpec(memory_space=pltpu.VMEM),
        scratch_shapes=[
            pltpu.SMEM((2, NPHASE), F32),
            pltpu.VMEM((COMPS, XW, 16, 128), BF16),
            pltpu.VMEM((XW, 16, 128), jnp.int32),
            pltpu.VMEM((2 * NY, 2 * NY), BF16),
            pltpu.VMEM((512, 512), BF16),
            pltpu.VMEM((2, 16, 128), F32),
            pltpu.VMEM((8, 256, 256), BF16),
            pltpu.VMEM((2, 16, 128), F32),
            pltpu.VMEM((2, 8, 128), F32),
            pltpu.VMEM((XW, 16, 128), F32),
            pltpu.VMEM((32 * UNITS, 128), BF16),
            pltpu.VMEM((32 * PENCIL, 128), BF16),
            pltpu.VMEM((32 * PENCIL, 128), BF16),
            pltpu.VMEM((32 * SLAB, 128), BF16),
            pltpu.VMEM((32 * SLAB, 128), BF16),
            pltpu.VMEM((32 * UNITS, 128), BF16),
            pltpu.SemaphoreType.DMA((3,)),
            pltpu.SemaphoreType.DMA((6,)),
            pltpu.SemaphoreType.DMA((3,)),
            pltpu.SemaphoreType.DMA((3,)),
        ],
        compiler_params=pltpu.CompilerParams(
            collective_id=0, has_side_effects=True, vmem_limit_bytes=32 * 1024 * 1024
        ),
    )(moduli, strain, labels, *consts)


def solution(mesh):
    return jax.shard_map(
        per_device,
        mesh=mesh,
        in_specs=(P(None, None, "pencil", "slab"), P(None, "pencil", "slab"), P()),
        out_specs=P(None, None, None, "pencil", "slab"),
        check_vma=False,
    )
```

```python
import math

import jax
import jax.numpy as jnp
import numpy as np
from jax import lax
from jax.experimental import pallas as pl
from jax.experimental.pallas import tpu as pltpu
from jax.sharding import PartitionSpec as P

MESH = pl.DeviceIdType.MESH
NX, NY, NZ = 2048, 512, 2048
XW, MODES, KX0, NPHASE, COMPS = 16, 2, 64, 4, 6
PENCIL, SLAB = 32, 16
UNITS = 12
SLAB_ORDER = (0, 1, 2, 3, 14, 15, 4, 5, 12, 13, 6, 7, 10, 11, 8, 9)
Q_FLOOR = 0.01
F32, BF16 = jnp.float32, jnp.bfloat16


def wrap(index, size):
    return jnp.where(index >= size, index - size, index)


def z_place(unit, owner):
    return wrap(wrap(unit + 5 * owner % UNITS, UNITS) + SLAB - 4, SLAB)


def z_unit(place, owner):
    return lax.rem(wrap(place + 4, SLAB) + 13 * UNITS - 5 * owner, UNITS)


def far_first(chips, each):
    order = sorted(range(chips), key=lambda step: -min(step, chips - step))
    return [chip * each + i for chip in order for i in reversed(range(each))]


def parts_table(angle):
    cosine, sine = np.cos(angle), np.sin(angle)
    return np.stack([np.stack([cosine, sine], 1), np.stack([-sine, cosine], 1)])


def tables():
    angle = 2 * math.pi / NY * (np.outer(np.arange(NY), np.arange(NY)) % NY)
    along_y = parts_table(angle).reshape(2, PENCIL, 16, 2, PENCIL, 16)
    along_y = along_y.transpose(1, 0, 2, 4, 3, 5).reshape(2 * NY, 2 * NY)
    angle = 2 * math.pi / 16 * (np.outer(np.arange(16), np.arange(16)) % 16)
    coarse = np.einsum("obrs,kj->okbsrj", parts_table(angle), np.eye(16)).reshape(512, 512)
    angle = 2 * math.pi / NZ * np.outer(np.arange(16), np.arange(128))
    turn = np.stack([np.cos(angle), np.sin(angle)]) / math.sqrt(NZ)
    angle = 2 * math.pi / 128 * (np.outer(np.arange(128), np.arange(128)) % 128)
    fine = parts_table(angle).reshape(2, SLAB, 8, 256)[:, list(SLAB_ORDER)].transpose(1, 0, 2, 3)
    fine = fine.reshape(256, 256)
    angle = math.pi / NY * np.arange(NY).reshape(PENCIL, 16, 1)
    angle = np.broadcast_to(angle, (PENCIL, 16, 128))
    freq_y = np.stack([np.sin(angle), np.cos(angle)], 1)
    angle = math.pi / NZ * np.arange(NZ).reshape(SLAB, 1, 128)
    angle = np.broadcast_to(angle, (SLAB, 8, 128))
    freq_z = np.stack([np.sin(angle), np.cos(angle)], 1)
    return (
        along_y.astype(BF16),
        coarse.astype(BF16),
        turn.astype(np.float32),
        fine.astype(BF16),
        freq_y.astype(np.float32),
        freq_z.astype(np.float32),
    )


def transform_z(data, coarse, turn):
    mixed = jnp.dot(coarse, data, preferred_element_type=F32).reshape(2, 16, 16, 128)
    cosine, sine = turn[0][None], turn[1][None]
    real = mixed[0] * cosine + mixed[1] * sine
    imag = mixed[1] * cosine - mixed[0] * sine
    parts = [part.reshape(256, 128).astype(BF16) for part in (real, imag)]
    return jnp.concatenate(parts, 1)


def exchange_bit(values, axis, bit):
    size = values.shape[axis]
    if 2 * bit == size:
        return pltpu.roll(values, bit, axis)
    index = lax.broadcasted_iota(jnp.int32, values.shape, axis)
    return jnp.where((index & bit) != 0, pltpu.roll(values, bit, axis), pltpu.roll(values, size - bit, axis))


def last_points(band, fine):
    product = lax.dot_general(fine[...], band, (((1,), (1,)), ((), ())), preferred_element_type=F32)
    halves = []
    for half in range(2):
        values = product[:, 128 * half : 128 * half + 128].reshape(32, 8, 128)
        row = lax.broadcasted_iota(jnp.int32, values.shape, 1)
        block = lax.broadcasted_iota(jnp.int32, values.shape, 2) // 16
        for bit in (1, 2, 4):
            traded = exchange_bit(exchange_bit(values, 1, bit), 2, 16 * bit)
            values = jnp.where(((row ^ block) & bit) == 0, values, traded)
        halves.append(values.reshape(256, 128))
    return jnp.concatenate(halves, 1)


def contrast(labels, values, base, factor):
    levels = [(values[phase] - base) * factor for phase in range(NPHASE)]
    chosen = jnp.where(labels == 2, levels[2], levels[3])
    chosen = jnp.where(labels == 1, levels[1], chosen)
    return jnp.where(labels == 0, levels[0], chosen)


def wave(mode, plane):
    angle = 2 * math.pi / NX * ((KX0 + mode) * plane % NX)
    scale = 1 / math.sqrt(XW)
    return float(math.cos(angle) * scale), float(-math.sin(angle) * scale)


def kernel(
    moduli_hbm,
    strain_hbm,
    labels_hbm,
    along_y_hbm,
    coarse_hbm,
    turn_hbm,
    fine_hbm,
    freq_y_hbm,
    freq_z_hbm,
    out,
    moduli,
    strain,
    labels,
    along_y,
    coarse,
    turn,
    fine,
    freq_y,
    freq_z,
    shear,
    send1,
    land1,
    send2,
    land2,
    send3,
    land3,
    in_sems,
    table_sems,
    send_sems,
    land_sems,
):
    pencil = lax.axis_index("pencil")
    slab = lax.axis_index("slab")
    works_y = (pencil < 24) & (pencil % 2 == 0)
    unit_y = pencil // 4 * 2 + pencil % 4 // 2
    works_z = wrap(slab + 4, SLAB) < UNITS

    barrier = pltpu.get_barrier_semaphore()

    @pl.when(works_y)
    def _():
        for step in far_first(8, 4)[:-1]:
            other = wrap(pencil + step, PENCIL)
            pl.semaphore_signal(barrier, inc=1, device_id=(other, slab), device_id_type=MESH)

    @pl.when(works_z)
    def _():
        for step in far_first(8, 2)[:-1]:
            other = wrap(slab + step, SLAB)
            pl.semaphore_signal(barrier, inc=1, device_id=(pencil, other), device_id_type=MESH)

    moduli_load = pltpu.make_async_copy(moduli_hbm, moduli, in_sems.at[2])
    moduli_load.start()
    loads = [
        pltpu.make_async_copy(strain_hbm, strain, in_sems.at[0]),
        pltpu.make_async_copy(labels_hbm, labels, in_sems.at[1]),
    ]
    for load in loads:
        load.start()
    pairs = [
        (freq_y_hbm.at[pencil], freq_y),
        (freq_z_hbm.at[slab], freq_z),
        (along_y_hbm, along_y),
        (coarse_hbm, coarse),
        (turn_hbm, turn),
        (fine_hbm, fine),
    ]
    table_loads = [pltpu.make_async_copy(a, b, table_sems.at[i]) for i, (a, b) in enumerate(pairs)]
    for load in table_loads:
        load.start()

    moduli_load.wait()
    lam0 = 0.5 * (
        jnp.minimum(jnp.minimum(moduli[0, 0], moduli[0, 1]), jnp.minimum(moduli[0, 2], moduli[0, 3]))
        + jnp.maximum(jnp.maximum(moduli[0, 0], moduli[0, 1]), jnp.maximum(moduli[0, 2], moduli[0, 3]))
    )
    mu0 = 0.5 * (
        jnp.minimum(jnp.minimum(moduli[1, 0], moduli[1, 1]), jnp.minimum(moduli[1, 2], moduli[1, 3]))
        + jnp.maximum(jnp.maximum(moduli[1, 0], moduli[1, 1]), jnp.maximum(moduli[1, 2], moduli[1, 3]))
    )

    for load in loads:
        load.wait()

    def emit(comp, mode, real, imag):
        start = 32 * (2 * comp + mode)
        send1[start : start + 16, :] = real.astype(BF16)
        send1[start + 16 : start + 32, :] = imag.astype(BF16)

    def add(total, term):
        return term if total is None else total + term

    level_lam = [moduli[0, phase] for phase in range(NPHASE)]
    level_mu = [moduli[1, phase] for phase in range(NPHASE)]
    shared = [[None, None] for _ in range(MODES)]
    sums = [[[None, None] for _ in range(MODES)] for _ in range(3)]
    for plane in range(XW):
        phases = labels[plane]
        shift_lam = contrast(phases, level_lam, lam0, 1.0)
        shift_mu = contrast(phases, level_mu, mu0, 2.0)
        shear[plane] = shift_mu
        parts = [strain[comp, plane].astype(F32) for comp in range(3)]
        trace = shift_lam * (parts[0] + parts[1] + parts[2])
        parts = [shift_mu * part for part in parts]
        for mode in range(MODES):
            for side, weight in enumerate(wave(mode, plane)):
                if weight == 0.0:
                    continue
                shared[mode][side] = add(shared[mode][side], weight * trace)
                for comp in range(3):
                    sums[comp][mode][side] = add(sums[comp][mode][side], weight * parts[comp])
    for comp in range(3):
        for mode in range(MODES):
            emit(comp, mode, sums[comp][mode][0] + shared[mode][0], sums[comp][mode][1] + shared[mode][1])
    sums = [[[None, None] for _ in range(MODES)] for _ in range(3)]
    for plane in range(XW):
        shift_mu = shear[plane]
        parts = [shift_mu * strain[3 + comp, plane].astype(F32) for comp in range(3)]
        for mode in range(MODES):
            for side, weight in enumerate(wave(mode, plane)):
                if weight == 0.0:
                    continue
                for comp in range(3):
                    sums[comp][mode][side] = add(sums[comp][mode][side], weight * parts[comp])
    for comp in range(3):
        for mode in range(MODES):
            emit(3 + comp, mode, sums[comp][mode][0], sums[comp][mode][1])

    greetings = jnp.where(works_y, UNITS - 1, UNITS) + jnp.where(works_z, UNITS - 1, UNITS)
    pl.semaphore_wait(barrier, greetings)

    def tile(index):
        return pl.ds(pl.multiple_of(index * 32, 32), 32)

    for unit in (10, 11, 8, 9, 6, 7, 4, 5, 2, 3, 0, 1):
        place = 4 * (unit // 2) + 2 * (unit % 2)

        @pl.when(pencil != place)
        def _():
            pltpu.make_async_remote_copy(
                src_ref=send1.at[tile(unit)],
                dst_ref=land1.at[tile(pencil)],
                send_sem=send_sems.at[0],
                recv_sem=land_sems.at[0],
                device_id=(place, slab),
                device_id_type=MESH,
            ).start()

    @pl.when(works_y)
    def _():
        pltpu.make_async_copy(send1.at[tile(unit_y)], land1.at[tile(pencil)], land_sems.at[0]).start()

    for load in table_loads[:2]:
        load.wait()
    sin_y, cos_y = freq_y[0], freq_y[1]
    sin_z, cos_z = (jnp.tile(freq_z[i], (2, 1)) for i in range(2))
    cos_yz, sin_cos, cos_sin = cos_y * cos_z, sin_y * cos_z, cos_y * sin_z

    def exchange_2(owner, own):
        mine = z_place(unit_y, owner)
        source = send2.at[tile(owner)]
        target = land2.at[tile(slab)]
        if own:
            pltpu.make_async_copy(source, target, land_sems.at[1]).start()
        else:
            pltpu.make_async_remote_copy(
                src_ref=source,
                dst_ref=target,
                send_sem=send_sems.at[1],
                recv_sem=land_sems.at[1],
                device_id=(owner, mine),
                device_id_type=MESH,
            ).start()

    stays = works_z & (z_unit(slab, pencil) == unit_y)

    @pl.when(works_y)
    def _():
        table_loads[2].wait()
        pltpu.make_async_copy(land1, land1, land_sems.at[0]).wait()
        for begin, end in ((0, 4), (4, 8), (8, 16), (16, 24), (24, 32)):
            rows = slice(32 * begin, 32 * end)
            band = jnp.dot(along_y[rows, :], land1[...], preferred_element_type=F32)
            send2[rows, :] = (band * (1 / math.sqrt(NY))).astype(BF16)
            for owner in range(begin, end):
                if owner % 2 or owner >= 2 * UNITS:
                    exchange_2(owner, False)
                    continue
                own = stays & (pencil == owner)

                @pl.when(own)
                def _():
                    exchange_2(owner, True)

                @pl.when(jnp.logical_not(own))
                def _():
                    exchange_2(owner, False)

    for load in table_loads[3:]:
        load.wait()

    @pl.when(jnp.logical_not(works_y))
    def _():
        table_loads[2].wait()

    @pl.when(works_z)
    def _():
        unit = z_unit(slab, pencil)
        pltpu.make_async_copy(land2, land2, land_sems.at[1]).wait()
        band = transform_z(land2[...], coarse[...], turn)
        points = last_points(band, fine)
        for place, owner in enumerate(SLAB_ORDER):
            for part in range(2):
                row, start = 16 * place + 8 * part, 32 * owner + 16 * part
                halves = [points[row : row + 8, 128 * half : 128 * half + 128] for half in range(2)]
                send3[start : start + 16, :] = jnp.concatenate(halves, 0).astype(BF16)
        for owner in SLAB_ORDER:
            source, target = send3.at[tile(owner)], land3.at[tile(unit)]

            @pl.when(slab == owner)
            def _():
                pltpu.make_async_copy(source, target, land_sems.at[2]).start()

            @pl.when(slab != owner)
            def _():
                pltpu.make_async_remote_copy(
                    src_ref=source,
                    dst_ref=target,
                    send_sem=send_sems.at[2],
                    recv_sem=land_sems.at[2],
                    device_id=(pencil, owner),
                    device_id_type=MESH,
                ).start()

    factor = (lam0 + mu0) / (mu0 * (lam0 + 2.0 * mu0))
    half_mu = 1.0 / (2.0 * mu0)
    weights = []
    for mode in range(MODES):
        angle = math.pi / NX * (KX0 + mode)
        sin_x, cos_x = math.sin(angle), math.cos(angle)
        qx, qy, qz = sin_x * cos_yz, cos_x * sin_cos, cos_x * cos_sin
        inverse = 1.0 / jnp.maximum(qx * qx + qy * qy + qz * qz, Q_FLOOR)
        weights.append((qx, qy, qz, half_mu * inverse, factor * inverse * inverse))
    pltpu.make_async_copy(land3, land3, land_sems.at[2]).wait()
    for mode in range(MODES):
        qx, qy, qz, first, second = weights[mode]
        for part in range(2):
            spectrum = []
            for comp in range(COMPS):
                start = 32 * (2 * comp + mode) + 16 * part
                spectrum.append(land3[start : start + 16, :].astype(F32))
            txx, tyy, tzz, tyz, txz, txy = spectrum
            vecx = txx * qx + txy * qy + txz * qz
            vecy = txy * qx + tyy * qy + tyz * qz
            vecz = txz * qx + tyz * qy + tzz * qz
            inner = second * (qx * vecx + qy * vecy + qz * vecz)
            vecx, vecy, vecz = first * vecx, first * vecy, first * vecz
            out[0, part, mode] = qx * (inner * qx - 2.0 * vecx)
            out[1, part, mode] = qy * (inner * qy - 2.0 * vecy)
            out[2, part, mode] = qz * (inner * qz - 2.0 * vecz)
            out[3, part, mode] = inner * qy * qz - (qy * vecz + qz * vecy)
            out[4, part, mode] = inner * qx * qz - (qx * vecz + qz * vecx)
            out[5, part, mode] = inner * qx * qy - (qx * vecy + qy * vecx)

    @pl.when(works_y)
    def _():
        gone = send1.at[pl.ds(0, 32 * (UNITS - 1))]
        pltpu.make_async_copy(gone, gone, send_sems.at[0]).wait()

        @pl.when(stays)
        def _():
            gone = send2.at[pl.ds(0, 32 * (PENCIL - 1))]
            pltpu.make_async_copy(gone, gone, send_sems.at[1]).wait()

        @pl.when(jnp.logical_not(stays))
        def _():
            pltpu.make_async_copy(send2, send2, send_sems.at[1]).wait()

    @pl.when(jnp.logical_not(works_y))
    def _():
        pltpu.make_async_copy(send1, send1, send_sems.at[0]).wait()

    @pl.when(works_z)
    def _():
        gone = send3.at[pl.ds(0, 32 * (SLAB - 1))]
        pltpu.make_async_copy(gone, gone, send_sems.at[2]).wait()


def per_device(strain, labels, moduli):
    consts = [jnp.asarray(const) for const in tables()]
    moduli, strain, labels, *consts = [
        pltpu.with_memory_space_constraint(x, pltpu.HBM) for x in (moduli, strain, labels, *consts)
    ]
    anywhere = pl.BlockSpec(memory_space=pltpu.HBM)
    return pl.pallas_call(
        kernel,
        out_shape=jax.ShapeDtypeStruct((COMPS, 2, MODES, 16, 128), F32),
        in_specs=[anywhere] * 9,
        out_specs=pl.BlockSpec(memory_space=pltpu.VMEM),
        scratch_shapes=[
            pltpu.SMEM((2, NPHASE), F32),
            pltpu.VMEM((COMPS, XW, 16, 128), BF16),
            pltpu.VMEM((XW, 16, 128), jnp.int32),
            pltpu.VMEM((2 * NY, 2 * NY), BF16),
            pltpu.VMEM((512, 512), BF16),
            pltpu.VMEM((2, 16, 128), F32),
            pltpu.VMEM((256, 256), BF16),
            pltpu.VMEM((2, 16, 128), F32),
            pltpu.VMEM((2, 8, 128), F32),
            pltpu.VMEM((XW, 16, 128), F32),
            pltpu.VMEM((32 * UNITS, 128), BF16),
            pltpu.VMEM((32 * PENCIL, 128), BF16),
            pltpu.VMEM((32 * PENCIL, 128), BF16),
            pltpu.VMEM((32 * SLAB, 128), BF16),
            pltpu.VMEM((32 * SLAB, 128), BF16),
            pltpu.VMEM((32 * UNITS, 128), BF16),
            pltpu.SemaphoreType.DMA((3,)),
            pltpu.SemaphoreType.DMA((6,)),
            pltpu.SemaphoreType.DMA((3,)),
            pltpu.SemaphoreType.DMA((3,)),
        ],
        compiler_params=pltpu.CompilerParams(
            collective_id=0, has_side_effects=True, vmem_limit_bytes=32 * 1024 * 1024
        ),
    )(moduli, strain, labels, *consts)


def solution(mesh):
    return jax.shard_map(
        per_device,
        mesh=mesh,
        in_specs=(P(None, None, "pencil", "slab"), P(None, "pencil", "slab"), P()),
        out_specs=P(None, None, None, "pencil", "slab"),
        check_vma=False,
    )
```

```python
import math

import jax
import jax.numpy as jnp
import numpy as np
from jax import lax
from jax.experimental import pallas as pl
from jax.experimental.pallas import tpu as pltpu
from jax.sharding import PartitionSpec as P

MESH = pl.DeviceIdType.MESH
NX, NY, NZ = 2048, 512, 2048
XW, MODES, KX0, NPHASE, COMPS = 16, 2, 64, 4, 6
PENCIL, SLAB = 32, 16
UNITS = 12
Y_PLACES = (0, 2, 5, 7, 8, 10, 13, 15, 16, 18, 21, 23)
SLAB_ORDER = (0, 1, 2, 3, 14, 15, 4, 5, 12, 13, 6, 7, 10, 11, 8, 9)
Q_FLOOR = 0.01
F32, BF16 = jnp.float32, jnp.bfloat16


def wrap(index, size):
    return jnp.where(index >= size, index - size, index)


def z_place(unit, owner):
    return wrap(wrap(unit + 5 * owner % UNITS, UNITS) + SLAB - 4, SLAB)


def z_unit(place, owner):
    return lax.rem(wrap(place + 4, SLAB) + 13 * UNITS - 5 * owner, UNITS)


def far_first(chips, each):
    order = sorted(range(chips), key=lambda step: -min(step, chips - step))
    return [chip * each + i for chip in order for i in reversed(range(each))]


def parts_table(angle):
    cosine, sine = np.cos(angle), np.sin(angle)
    return np.stack([np.stack([cosine, sine], 1), np.stack([-sine, cosine], 1)])


def tables():
    angle = 2 * math.pi / NY * (np.outer(np.arange(NY), np.arange(NY)) % NY)
    along_y = parts_table(angle).reshape(2, PENCIL, 16, 2, PENCIL, 16)
    along_y = along_y.transpose(1, 0, 2, 4, 3, 5).reshape(2 * NY, 2 * NY)
    angle = 2 * math.pi / 16 * (np.outer(np.arange(16), np.arange(16)) % 16)
    coarse = np.einsum("obrs,kj->okbsrj", parts_table(angle), np.eye(16)).reshape(512, 512)
    angle = 2 * math.pi / NZ * np.outer(np.arange(16), np.arange(128))
    turn = np.stack([np.cos(angle), np.sin(angle)]) / math.sqrt(NZ)
    angle = 2 * math.pi / 128 * (np.outer(np.arange(128), np.arange(128)) % 128)
    fine = parts_table(angle).reshape(2, SLAB, 8, 256)[:, list(SLAB_ORDER)].transpose(1, 0, 2, 3)
    fine = fine.reshape(256, 256)
    angle = math.pi / NY * np.arange(NY).reshape(PENCIL, 16, 1)
    angle = np.broadcast_to(angle, (PENCIL, 16, 128))
    freq_y = np.stack([np.sin(angle), np.cos(angle)], 1)
    angle = math.pi / NZ * np.arange(NZ).reshape(SLAB, 1, 128)
    angle = np.broadcast_to(angle, (SLAB, 8, 128))
    freq_z = np.stack([np.sin(angle), np.cos(angle)], 1)
    return (
        along_y.astype(BF16),
        coarse.astype(BF16),
        turn.astype(np.float32),
        fine.astype(BF16),
        freq_y.astype(np.float32),
        freq_z.astype(np.float32),
    )


def transform_z(data, coarse, turn):
    mixed = jnp.dot(coarse, data, preferred_element_type=F32).reshape(2, 16, 16, 128)
    cosine, sine = turn[0][None], turn[1][None]
    real = mixed[0] * cosine + mixed[1] * sine
    imag = mixed[1] * cosine - mixed[0] * sine
    parts = [part.reshape(256, 128).astype(BF16) for part in (real, imag)]
    return jnp.concatenate(parts, 1)


def exchange_bit(values, axis, bit):
    size = values.shape[axis]
    if 2 * bit == size:
        return pltpu.roll(values, bit, axis)
    index = lax.broadcasted_iota(jnp.int32, values.shape, axis)
    return jnp.where((index & bit) != 0, pltpu.roll(values, bit, axis), pltpu.roll(values, size - bit, axis))


def last_points(band, fine):
    product = lax.dot_general(fine[...], band, (((1,), (1,)), ((), ())), preferred_element_type=F32)
    halves = []
    for half in range(2):
        values = product[:, 128 * half : 128 * half + 128].reshape(32, 8, 128)
        row = lax.broadcasted_iota(jnp.int32, values.shape, 1)
        block = lax.broadcasted_iota(jnp.int32, values.shape, 2) // 16
        for bit in (1, 2, 4):
            traded = exchange_bit(exchange_bit(values, 1, bit), 2, 16 * bit)
            values = jnp.where(((row ^ block) & bit) == 0, values, traded)
        halves.append(values.reshape(256, 128))
    return jnp.concatenate(halves, 1)


def contrast(labels, values, base, factor):
    levels = [(values[phase] - base) * factor for phase in range(NPHASE)]
    chosen = jnp.where(labels == 2, levels[2], levels[3])
    chosen = jnp.where(labels == 1, levels[1], chosen)
    return jnp.where(labels == 0, levels[0], chosen)


def wave(mode, plane):
    angle = 2 * math.pi / NX * ((KX0 + mode) * plane % NX)
    scale = 1 / math.sqrt(XW)
    return float(math.cos(angle) * scale), float(-math.sin(angle) * scale)


def kernel(
    moduli_hbm,
    strain_hbm,
    labels_hbm,
    along_y_hbm,
    coarse_hbm,
    turn_hbm,
    fine_hbm,
    freq_y_hbm,
    freq_z_hbm,
    out,
    moduli,
    strain,
    labels,
    along_y,
    coarse,
    turn,
    fine,
    freq_y,
    freq_z,
    shear,
    send1,
    land1,
    send2,
    land2,
    send3,
    land3,
    in_sems,
    table_sems,
    send_sems,
    land_sems,
):
    pencil = lax.axis_index("pencil")
    slab = lax.axis_index("slab")
    unit_y = sum(jnp.where(pencil == place, unit, 0) for unit, place in enumerate(Y_PLACES))
    works_y = sum(jnp.where(pencil == place, 1, 0) for place in Y_PLACES) > 0
    works_z = wrap(slab + 4, SLAB) < UNITS

    barrier = pltpu.get_barrier_semaphore()

    @pl.when(works_y)
    def _():
        for step in far_first(8, 4)[:-1]:
            other = wrap(pencil + step, PENCIL)
            pl.semaphore_signal(barrier, inc=1, device_id=(other, slab), device_id_type=MESH)

    @pl.when(works_z)
    def _():
        for step in far_first(8, 2)[:-1]:
            other = wrap(slab + step, SLAB)
            pl.semaphore_signal(barrier, inc=1, device_id=(pencil, other), device_id_type=MESH)

    moduli_load = pltpu.make_async_copy(moduli_hbm, moduli, in_sems.at[2])
    moduli_load.start()
    loads = [
        pltpu.make_async_copy(strain_hbm, strain, in_sems.at[0]),
        pltpu.make_async_copy(labels_hbm, labels, in_sems.at[1]),
    ]
    for load in loads:
        load.start()
    pairs = [
        (freq_y_hbm.at[pencil], freq_y),
        (freq_z_hbm.at[slab], freq_z),
        (along_y_hbm, along_y),
        (coarse_hbm, coarse),
        (turn_hbm, turn),
        (fine_hbm, fine),
    ]
    table_loads = [pltpu.make_async_copy(a, b, table_sems.at[i]) for i, (a, b) in enumerate(pairs)]
    for load in table_loads:
        load.start()

    moduli_load.wait()
    lam0 = 0.5 * (
        jnp.minimum(jnp.minimum(moduli[0, 0], moduli[0, 1]), jnp.minimum(moduli[0, 2], moduli[0, 3]))
        + jnp.maximum(jnp.maximum(moduli[0, 0], moduli[0, 1]), jnp.maximum(moduli[0, 2], moduli[0, 3]))
    )
    mu0 = 0.5 * (
        jnp.minimum(jnp.minimum(moduli[1, 0], moduli[1, 1]), jnp.minimum(moduli[1, 2], moduli[1, 3]))
        + jnp.maximum(jnp.maximum(moduli[1, 0], moduli[1, 1]), jnp.maximum(moduli[1, 2], moduli[1, 3]))
    )

    for load in loads:
        load.wait()

    def emit(comp, mode, real, imag):
        start = 32 * (2 * comp + mode)
        send1[start : start + 16, :] = real.astype(BF16)
        send1[start + 16 : start + 32, :] = imag.astype(BF16)

    def add(total, term):
        return term if total is None else total + term

    level_lam = [moduli[0, phase] for phase in range(NPHASE)]
    level_mu = [moduli[1, phase] for phase in range(NPHASE)]
    shared = [[None, None] for _ in range(MODES)]
    sums = [[[None, None] for _ in range(MODES)] for _ in range(3)]
    for plane in range(XW):
        phases = labels[plane]
        shift_lam = contrast(phases, level_lam, lam0, 1.0)
        shift_mu = contrast(phases, level_mu, mu0, 2.0)
        shear[plane] = shift_mu
        parts = [strain[comp, plane].astype(F32) for comp in range(3)]
        trace = shift_lam * (parts[0] + parts[1] + parts[2])
        parts = [shift_mu * part for part in parts]
        for mode in range(MODES):
            for side, weight in enumerate(wave(mode, plane)):
                if weight == 0.0:
                    continue
                shared[mode][side] = add(shared[mode][side], weight * trace)
                for comp in range(3):
                    sums[comp][mode][side] = add(sums[comp][mode][side], weight * parts[comp])
    for comp in range(3):
        for mode in range(MODES):
            emit(comp, mode, sums[comp][mode][0] + shared[mode][0], sums[comp][mode][1] + shared[mode][1])
    sums = [[[None, None] for _ in range(MODES)] for _ in range(3)]
    for plane in range(XW):
        shift_mu = shear[plane]
        parts = [shift_mu * strain[3 + comp, plane].astype(F32) for comp in range(3)]
        for mode in range(MODES):
            for side, weight in enumerate(wave(mode, plane)):
                if weight == 0.0:
                    continue
                for comp in range(3):
                    sums[comp][mode][side] = add(sums[comp][mode][side], weight * parts[comp])
    for comp in range(3):
        for mode in range(MODES):
            emit(3 + comp, mode, sums[comp][mode][0], sums[comp][mode][1])

    greetings = jnp.where(works_y, UNITS - 1, UNITS) + jnp.where(works_z, UNITS - 1, UNITS)
    pl.semaphore_wait(barrier, greetings)

    def tile(index):
        return pl.ds(pl.multiple_of(index * 32, 32), 32)

    for unit in reversed(range(UNITS)):
        place = Y_PLACES[unit]

        @pl.when(pencil != place)
        def _():
            pltpu.make_async_remote_copy(
                src_ref=send1.at[tile(unit)],
                dst_ref=land1.at[tile(pencil)],
                send_sem=send_sems.at[0],
                recv_sem=land_sems.at[0],
                device_id=(place, slab),
                device_id_type=MESH,
            ).start()

    @pl.when(works_y)
    def _():
        pltpu.make_async_copy(send1.at[tile(unit_y)], land1.at[tile(pencil)], land_sems.at[0]).start()

    for load in table_loads[:2]:
        load.wait()
    sin_y, cos_y = freq_y[0], freq_y[1]
    sin_z, cos_z = (jnp.tile(freq_z[i], (2, 1)) for i in range(2))
    cos_yz, sin_cos, cos_sin = cos_y * cos_z, sin_y * cos_z, cos_y * sin_z

    def exchange_2(owner, own):
        mine = z_place(unit_y, owner)
        source = send2.at[tile(owner)]
        target = land2.at[tile(slab)]
        if own:
            pltpu.make_async_copy(source, target, land_sems.at[1]).start()
        else:
            pltpu.make_async_remote_copy(
                src_ref=source,
                dst_ref=target,
                send_sem=send_sems.at[1],
                recv_sem=land_sems.at[1],
                device_id=(owner, mine),
                device_id_type=MESH,
            ).start()

    stays = works_z & (z_unit(slab, pencil) == unit_y)

    @pl.when(works_y)
    def _():
        table_loads[2].wait()
        pltpu.make_async_copy(land1, land1, land_sems.at[0]).wait()
        for begin, end in ((0, 4), (4, 8), (8, 16), (16, 24), (24, 32)):
            rows = slice(32 * begin, 32 * end)
            band = jnp.dot(along_y[rows, :], land1[...], preferred_element_type=F32)
            send2[rows, :] = (band * (1 / math.sqrt(NY))).astype(BF16)
            for owner in range(begin, end):
                if owner not in Y_PLACES:
                    exchange_2(owner, False)
                    continue
                own = stays & (pencil == owner)

                @pl.when(own)
                def _():
                    exchange_2(owner, True)

                @pl.when(jnp.logical_not(own))
                def _():
                    exchange_2(owner, False)

    for load in table_loads[3:]:
        load.wait()

    @pl.when(jnp.logical_not(works_y))
    def _():
        table_loads[2].wait()

    @pl.when(works_z)
    def _():
        unit = z_unit(slab, pencil)
        pltpu.make_async_copy(land2, land2, land_sems.at[1]).wait()
        band = transform_z(land2[...], coarse[...], turn)
        points = last_points(band, fine)
        for place, owner in enumerate(SLAB_ORDER):
            for part in range(2):
                row, start = 16 * place + 8 * part, 32 * owner + 16 * part
                halves = [points[row : row + 8, 128 * half : 128 * half + 128] for half in range(2)]
                send3[start : start + 16, :] = jnp.concatenate(halves, 0).astype(BF16)
        for owner in SLAB_ORDER:
            source, target = send3.at[tile(owner)], land3.at[tile(unit)]

            @pl.when(slab == owner)
            def _():
                pltpu.make_async_copy(source, target, land_sems.at[2]).start()

            @pl.when(slab != owner)
            def _():
                pltpu.make_async_remote_copy(
                    src_ref=source,
                    dst_ref=target,
                    send_sem=send_sems.at[2],
                    recv_sem=land_sems.at[2],
                    device_id=(pencil, owner),
                    device_id_type=MESH,
                ).start()

    factor = (lam0 + mu0) / (mu0 * (lam0 + 2.0 * mu0))
    half_mu = 1.0 / (2.0 * mu0)
    weights = []
    for mode in range(MODES):
        angle = math.pi / NX * (KX0 + mode)
        sin_x, cos_x = math.sin(angle), math.cos(angle)
        qx, qy, qz = sin_x * cos_yz, cos_x * sin_cos, cos_x * cos_sin
        inverse = 1.0 / jnp.maximum(qx * qx + qy * qy + qz * qz, Q_FLOOR)
        weights.append((qx, qy, qz, half_mu * inverse, factor * inverse * inverse))
    pltpu.make_async_copy(land3, land3, land_sems.at[2]).wait()
    for mode in range(MODES):
        qx, qy, qz, first, second = weights[mode]
        for part in range(2):
            spectrum = []
            for comp in range(COMPS):
                start = 32 * (2 * comp + mode) + 16 * part
                spectrum.append(land3[start : start + 16, :].astype(F32))
            txx, tyy, tzz, tyz, txz, txy = spectrum
            vecx = txx * qx + txy * qy + txz * qz
            vecy = txy * qx + tyy * qy + tyz * qz
            vecz = txz * qx + tyz * qy + tzz * qz
            inner = second * (qx * vecx + qy * vecy + qz * vecz)
            vecx, vecy, vecz = first * vecx, first * vecy, first * vecz
            out[0, part, mode] = qx * (inner * qx - 2.0 * vecx)
            out[1, part, mode] = qy * (inner * qy - 2.0 * vecy)
            out[2, part, mode] = qz * (inner * qz - 2.0 * vecz)
            out[3, part, mode] = inner * qy * qz - (qy * vecz + qz * vecy)
            out[4, part, mode] = inner * qx * qz - (qx * vecz + qz * vecx)
            out[5, part, mode] = inner * qx * qy - (qx * vecy + qy * vecx)

    @pl.when(works_y)
    def _():
        gone = send1.at[pl.ds(0, 32 * (UNITS - 1))]
        pltpu.make_async_copy(gone, gone, send_sems.at[0]).wait()

        @pl.when(stays)
        def _():
            gone = send2.at[pl.ds(0, 32 * (PENCIL - 1))]
            pltpu.make_async_copy(gone, gone, send_sems.at[1]).wait()

        @pl.when(jnp.logical_not(stays))
        def _():
            pltpu.make_async_copy(send2, send2, send_sems.at[1]).wait()

    @pl.when(jnp.logical_not(works_y))
    def _():
        pltpu.make_async_copy(send1, send1, send_sems.at[0]).wait()

    @pl.when(works_z)
    def _():
        gone = send3.at[pl.ds(0, 32 * (SLAB - 1))]
        pltpu.make_async_copy(gone, gone, send_sems.at[2]).wait()


def per_device(strain, labels, moduli):
    consts = [jnp.asarray(const) for const in tables()]
    moduli, strain, labels, *consts = [
        pltpu.with_memory_space_constraint(x, pltpu.HBM) for x in (moduli, strain, labels, *consts)
    ]
    anywhere = pl.BlockSpec(memory_space=pltpu.HBM)
    return pl.pallas_call(
        kernel,
        out_shape=jax.ShapeDtypeStruct((COMPS, 2, MODES, 16, 128), F32),
        in_specs=[anywhere] * 9,
        out_specs=pl.BlockSpec(memory_space=pltpu.VMEM),
        scratch_shapes=[
            pltpu.SMEM((2, NPHASE), F32),
            pltpu.VMEM((COMPS, XW, 16, 128), BF16),
            pltpu.VMEM((XW, 16, 128), jnp.int32),
            pltpu.VMEM((2 * NY, 2 * NY), BF16),
            pltpu.VMEM((512, 512), BF16),
            pltpu.VMEM((2, 16, 128), F32),
            pltpu.VMEM((256, 256), BF16),
            pltpu.VMEM((2, 16, 128), F32),
            pltpu.VMEM((2, 8, 128), F32),
            pltpu.VMEM((XW, 16, 128), F32),
            pltpu.VMEM((32 * UNITS, 128), BF16),
            pltpu.VMEM((32 * PENCIL, 128), BF16),
            pltpu.VMEM((32 * PENCIL, 128), BF16),
            pltpu.VMEM((32 * SLAB, 128), BF16),
            pltpu.VMEM((32 * SLAB, 128), BF16),
            pltpu.VMEM((32 * UNITS, 128), BF16),
            pltpu.SemaphoreType.DMA((3,)),
            pltpu.SemaphoreType.DMA((6,)),
            pltpu.SemaphoreType.DMA((3,)),
            pltpu.SemaphoreType.DMA((3,)),
        ],
        compiler_params=pltpu.CompilerParams(
            collective_id=0, has_side_effects=True, vmem_limit_bytes=32 * 1024 * 1024
        ),
    )(moduli, strain, labels, *consts)


def solution(mesh):
    return jax.shard_map(
        per_device,
        mesh=mesh,
        in_specs=(P(None, None, "pencil", "slab"), P(None, "pencil", "slab"), P()),
        out_specs=P(None, None, None, "pencil", "slab"),
        check_vma=False,
    )
```

```python
import math

import jax
import jax.numpy as jnp
import numpy as np
from jax import lax
from jax.experimental import pallas as pl
from jax.experimental.pallas import tpu as pltpu
from jax.sharding import PartitionSpec as P

MESH = pl.DeviceIdType.MESH
NX, NY, NZ = 2048, 512, 2048
XW, MODES, KX0, NPHASE, COMPS = 16, 2, 64, 4, 6
PENCIL, SLAB = 32, 16
UNITS = 12
Y_PLACES = (0, 2, 5, 7, 8, 10, 13, 15, 24, 26, 29, 31)
SLAB_ORDER = (0, 1, 2, 3, 4, 5, 14, 15, 6, 7, 12, 13, 8, 9, 10, 11)
Q_FLOOR = 0.01
F32, BF16 = jnp.float32, jnp.bfloat16


def wrap(index, size):
    return jnp.where(index >= size, index - size, index)


def z_place(unit, owner):
    return wrap(wrap(unit + 5 * owner % UNITS, UNITS) + SLAB - 4, SLAB)


def z_unit(place, owner):
    return lax.rem(wrap(place + 4, SLAB) + 13 * UNITS - 5 * owner, UNITS)


def far_first(chips, each):
    order = sorted(range(chips), key=lambda step: -min(step, chips - step))
    return [chip * each + i for chip in order for i in reversed(range(each))]


def parts_table(angle):
    cosine, sine = np.cos(angle), np.sin(angle)
    return np.stack([np.stack([cosine, sine], 1), np.stack([-sine, cosine], 1)])


def tables():
    angle = 2 * math.pi / NY * (np.outer(np.arange(NY), np.arange(NY)) % NY)
    along_y = parts_table(angle).reshape(2, PENCIL, 16, 2, PENCIL, 16)
    along_y = along_y.transpose(1, 0, 2, 4, 3, 5).reshape(2 * NY, 2 * NY)
    angle = 2 * math.pi / 16 * (np.outer(np.arange(16), np.arange(16)) % 16)
    coarse = np.einsum("obrs,kj->okbsrj", np.roll(parts_table(angle), 4, 3), np.eye(16)).reshape(512, 512)
    angle = 2 * math.pi / NZ * np.outer(np.arange(16), np.arange(128))
    turn = np.stack([np.cos(angle), np.sin(angle)]) / math.sqrt(NZ)
    angle = 2 * math.pi / 128 * (np.outer(np.arange(128), np.arange(128)) % 128)
    fine = parts_table(angle).reshape(2, SLAB, 8, 256)[:, list(SLAB_ORDER)].transpose(1, 0, 2, 3)
    fine = fine.reshape(256, 256)
    angle = math.pi / NY * np.arange(NY).reshape(PENCIL, 16, 1)
    angle = np.broadcast_to(angle, (PENCIL, 16, 128))
    freq_y = np.stack([np.sin(angle), np.cos(angle)], 1)
    angle = math.pi / NZ * np.arange(NZ).reshape(SLAB, 1, 128)
    angle = np.broadcast_to(angle, (SLAB, 8, 128))
    freq_z = np.stack([np.sin(angle), np.cos(angle)], 1)
    return (
        along_y.astype(BF16),
        coarse.astype(BF16),
        turn.astype(np.float32),
        fine.astype(BF16),
        freq_y.astype(np.float32),
        freq_z.astype(np.float32),
    )


def turn_z(mixed, turn):
    mixed = mixed.reshape(2, 16, 16, 128)
    cosine, sine = turn[0][None], turn[1][None]
    real = mixed[0] * cosine + mixed[1] * sine
    imag = mixed[1] * cosine - mixed[0] * sine
    parts = [part.reshape(256, 128).astype(BF16) for part in (real, imag)]
    return jnp.concatenate(parts, 1)


def exchange_bit(values, axis, bit):
    size = values.shape[axis]
    if 2 * bit == size:
        return pltpu.roll(values, bit, axis)
    index = lax.broadcasted_iota(jnp.int32, values.shape, axis)
    return jnp.where((index & bit) != 0, pltpu.roll(values, bit, axis), pltpu.roll(values, size - bit, axis))


def last_points(band, fine):
    product = lax.dot_general(fine[...], band, (((1,), (1,)), ((), ())), preferred_element_type=F32)
    halves = []
    for half in range(2):
        values = product[:, 128 * half : 128 * half + 128].reshape(32, 8, 128)
        row = lax.broadcasted_iota(jnp.int32, values.shape, 1)
        block = lax.broadcasted_iota(jnp.int32, values.shape, 2) // 16
        for bit in (1, 2, 4):
            traded = exchange_bit(exchange_bit(values, 1, bit), 2, 16 * bit)
            values = jnp.where(((row ^ block) & bit) == 0, values, traded)
        halves.append(values.reshape(256, 128))
    return jnp.concatenate(halves, 1)


def contrast(labels, values, base, factor):
    levels = [(values[phase] - base) * factor for phase in range(NPHASE)]
    chosen = jnp.where(labels == 2, levels[2], levels[3])
    chosen = jnp.where(labels == 1, levels[1], chosen)
    return jnp.where(labels == 0, levels[0], chosen)


def wave(mode, plane):
    angle = 2 * math.pi / NX * ((KX0 + mode) * plane % NX)
    scale = 1 / math.sqrt(XW)
    return float(math.cos(angle) * scale), float(-math.sin(angle) * scale)


def kernel(
    moduli_hbm,
    strain_hbm,
    labels_hbm,
    along_y_hbm,
    coarse_hbm,
    turn_hbm,
    fine_hbm,
    freq_y_hbm,
    freq_z_hbm,
    out,
    moduli,
    strain,
    labels,
    along_y,
    coarse,
    turn,
    fine,
    freq_y,
    freq_z,
    shear,
    send1,
    land1,
    send2,
    land2,
    send3,
    land3,
    in_sems,
    table_sems,
    send_sems,
    land_sems,
):
    pencil = lax.axis_index("pencil")
    slab = lax.axis_index("slab")
    unit_y = sum(jnp.where(pencil == place, unit, 0) for unit, place in enumerate(Y_PLACES))
    works_y = sum(jnp.where(pencil == place, 1, 0) for place in Y_PLACES) > 0
    works_z = wrap(slab + 4, SLAB) < UNITS

    barrier = pltpu.get_barrier_semaphore()

    @pl.when(works_z)
    def _():
        for step in far_first(8, 2)[:-1]:
            other = wrap(slab + step, SLAB)
            pl.semaphore_signal(barrier, inc=1, device_id=(pencil, other), device_id_type=MESH)

    @pl.when(works_y)
    def _():
        for step in far_first(8, 4)[:-1]:
            other = wrap(pencil + step, PENCIL)
            pl.semaphore_signal(barrier, inc=1, device_id=(other, slab), device_id_type=MESH)

    moduli_load = pltpu.make_async_copy(moduli_hbm, moduli, in_sems.at[2])
    moduli_load.start()
    loads = [
        pltpu.make_async_copy(strain_hbm, strain, in_sems.at[0]),
        pltpu.make_async_copy(labels_hbm, labels, in_sems.at[1]),
    ]
    for load in loads:
        load.start()
    pairs = [
        (freq_y_hbm.at[pencil], freq_y),
        (freq_z_hbm.at[slab], freq_z),
        (along_y_hbm, along_y),
        (coarse_hbm, coarse),
        (turn_hbm, turn),
        (fine_hbm, fine),
    ]
    table_loads = [pltpu.make_async_copy(a, b, table_sems.at[i]) for i, (a, b) in enumerate(pairs)]
    for load in table_loads:
        load.start()

    moduli_load.wait()
    lam0 = 0.5 * (
        jnp.minimum(jnp.minimum(moduli[0, 0], moduli[0, 1]), jnp.minimum(moduli[0, 2], moduli[0, 3]))
        + jnp.maximum(jnp.maximum(moduli[0, 0], moduli[0, 1]), jnp.maximum(moduli[0, 2], moduli[0, 3]))
    )
    mu0 = 0.5 * (
        jnp.minimum(jnp.minimum(moduli[1, 0], moduli[1, 1]), jnp.minimum(moduli[1, 2], moduli[1, 3]))
        + jnp.maximum(jnp.maximum(moduli[1, 0], moduli[1, 1]), jnp.maximum(moduli[1, 2], moduli[1, 3]))
    )

    for load in loads:
        load.wait()

    def emit(comp, mode, real, imag):
        start = 32 * (2 * comp + mode)
        send1[start : start + 16, :] = real.astype(BF16)
        send1[start + 16 : start + 32, :] = imag.astype(BF16)

    def add(total, term):
        return term if total is None else total + term

    level_lam = [moduli[0, phase] for phase in range(NPHASE)]
    level_mu = [moduli[1, phase] for phase in range(NPHASE)]
    shared = [[None, None] for _ in range(MODES)]
    sums = [[[None, None] for _ in range(MODES)] for _ in range(3)]
    for plane in range(XW):
        phases = labels[plane]
        shift_lam = contrast(phases, level_lam, lam0, 1.0)
        shift_mu = contrast(phases, level_mu, mu0, 2.0)
        shear[plane] = shift_mu
        parts = [strain[comp, plane].astype(F32) for comp in range(3)]
        trace = shift_lam * (parts[0] + parts[1] + parts[2])
        parts = [shift_mu * part for part in parts]
        for mode in range(MODES):
            for side, weight in enumerate(wave(mode, plane)):
                if weight == 0.0:
                    continue
                shared[mode][side] = add(shared[mode][side], weight * trace)
                for comp in range(3):
                    sums[comp][mode][side] = add(sums[comp][mode][side], weight * parts[comp])
    for comp in range(3):
        for mode in range(MODES):
            emit(comp, mode, sums[comp][mode][0] + shared[mode][0], sums[comp][mode][1] + shared[mode][1])
    sums = [[[None, None] for _ in range(MODES)] for _ in range(3)]
    for plane in range(XW):
        shift_mu = shear[plane]
        parts = [shift_mu * strain[3 + comp, plane].astype(F32) for comp in range(3)]
        for mode in range(MODES):
            for side, weight in enumerate(wave(mode, plane)):
                if weight == 0.0:
                    continue
                for comp in range(3):
                    sums[comp][mode][side] = add(sums[comp][mode][side], weight * parts[comp])
    for comp in range(3):
        for mode in range(MODES):
            emit(3 + comp, mode, sums[comp][mode][0], sums[comp][mode][1])

    greetings = jnp.where(works_y, UNITS - 1, UNITS) + jnp.where(works_z, UNITS - 1, UNITS)
    pl.semaphore_wait(barrier, greetings)

    def tile(index):
        return pl.ds(pl.multiple_of(index * 32, 32), 32)

    for unit in reversed(range(UNITS)):
        place = Y_PLACES[unit]

        @pl.when(pencil != place)
        def _():
            pltpu.make_async_remote_copy(
                src_ref=send1.at[tile(unit)],
                dst_ref=land1.at[tile(pencil)],
                send_sem=send_sems.at[0],
                recv_sem=land_sems.at[0],
                device_id=(place, slab),
                device_id_type=MESH,
            ).start()

    @pl.when(works_y)
    def _():
        pltpu.make_async_copy(send1.at[tile(unit_y)], land1.at[tile(pencil)], land_sems.at[0]).start()

    for load in table_loads[:2]:
        load.wait()
    sin_y, cos_y = freq_y[0], freq_y[1]
    sin_z, cos_z = (jnp.tile(freq_z[i], (2, 1)) for i in range(2))
    cos_yz, sin_cos, cos_sin = cos_y * cos_z, sin_y * cos_z, cos_y * sin_z

    arrival = jnp.where(wrap(slab + 4, SLAB) < SLAB // 2, 1, 3)

    def exchange_2(owner, own):
        mine = z_place(unit_y, owner)
        source = send2.at[tile(owner)]
        target = land2.at[tile(wrap(slab + 4, SLAB))]
        if own:
            pltpu.make_async_copy(source, target, land_sems.at[arrival]).start()
        else:
            pltpu.make_async_remote_copy(
                src_ref=source,
                dst_ref=target,
                send_sem=send_sems.at[1],
                recv_sem=land_sems.at[arrival],
                device_id=(owner, mine),
                device_id_type=MESH,
            ).start()

    stays = works_z & (z_unit(slab, pencil) == unit_y)

    @pl.when(works_y)
    def _():
        table_loads[2].wait()
        pltpu.make_async_copy(land1, land1, land_sems.at[0]).wait()
        for begin, end in ((0, 4), (4, 8), (8, 16), (16, 24), (24, 32)):
            rows = slice(32 * begin, 32 * end)
            band = jnp.dot(along_y[rows, :], land1[...], preferred_element_type=F32)
            send2[rows, :] = (band * (1 / math.sqrt(NY))).astype(BF16)
            for owner in range(begin, end):
                if owner not in Y_PLACES:
                    exchange_2(owner, False)
                    continue
                own = stays & (pencil == owner)

                @pl.when(own)
                def _():
                    exchange_2(owner, True)

                @pl.when(jnp.logical_not(own))
                def _():
                    exchange_2(owner, False)

    for load in table_loads[3:]:
        load.wait()

    @pl.when(jnp.logical_not(works_y))
    def _():
        table_loads[2].wait()

    @pl.when(works_z)
    def _():
        unit = z_unit(slab, pencil)
        mixed = None
        for slabs, arrived in ((slice(0, 256), 1), (slice(256, 512), 3)):
            pltpu.make_async_copy(land2.at[slabs], land2.at[slabs], land_sems.at[arrived]).wait()
            part = jnp.dot(coarse[:, slabs], land2[slabs, :], preferred_element_type=F32)
            mixed = part if mixed is None else mixed + part
        band = turn_z(mixed, turn)
        points = last_points(band, fine)
        for place, owner in enumerate(SLAB_ORDER):
            for part in range(2):
                row, start = 16 * place + 8 * part, 32 * owner + 16 * part
                halves = [points[row : row + 8, 128 * half : 128 * half + 128] for half in range(2)]
                send3[start : start + 16, :] = jnp.concatenate(halves, 0).astype(BF16)
        for owner in SLAB_ORDER:
            source, target = send3.at[tile(owner)], land3.at[tile(unit)]

            @pl.when(slab == owner)
            def _():
                pltpu.make_async_copy(source, target, land_sems.at[2]).start()

            @pl.when(slab != owner)
            def _():
                pltpu.make_async_remote_copy(
                    src_ref=source,
                    dst_ref=target,
                    send_sem=send_sems.at[2],
                    recv_sem=land_sems.at[2],
                    device_id=(pencil, owner),
                    device_id_type=MESH,
                ).start()

    factor = (lam0 + mu0) / (mu0 * (lam0 + 2.0 * mu0))
    half_mu = 1.0 / (2.0 * mu0)
    weights = []
    for mode in range(MODES):
        angle = math.pi / NX * (KX0 + mode)
        sin_x, cos_x = math.sin(angle), math.cos(angle)
        qx, qy, qz = sin_x * cos_yz, cos_x * sin_cos, cos_x * cos_sin
        inverse = 1.0 / jnp.maximum(qx * qx + qy * qy + qz * qz, Q_FLOOR)
        weights.append((qx, qy, qz, half_mu * inverse, factor * inverse * inverse))
    pltpu.make_async_copy(land3, land3, land_sems.at[2]).wait()
    for mode in range(MODES):
        qx, qy, qz, first, second = weights[mode]
        for part in range(2):
            spectrum = []
            for comp in range(COMPS):
                start = 32 * (2 * comp + mode) + 16 * part
                spectrum.append(land3[start : start + 16, :].astype(F32))
            txx, tyy, tzz, tyz, txz, txy = spectrum
            vecx = txx * qx + txy * qy + txz * qz
            vecy = txy * qx + tyy * qy + tyz * qz
            vecz = txz * qx + tyz * qy + tzz * qz
            inner = second * (qx * vecx + qy * vecy + qz * vecz)
            vecx, vecy, vecz = first * vecx, first * vecy, first * vecz
            out[0, part, mode] = qx * (inner * qx - 2.0 * vecx)
            out[1, part, mode] = qy * (inner * qy - 2.0 * vecy)
            out[2, part, mode] = qz * (inner * qz - 2.0 * vecz)
            out[3, part, mode] = inner * qy * qz - (qy * vecz + qz * vecy)
            out[4, part, mode] = inner * qx * qz - (qx * vecz + qz * vecx)
            out[5, part, mode] = inner * qx * qy - (qx * vecy + qy * vecx)

    @pl.when(works_y)
    def _():
        gone = send1.at[pl.ds(0, 32 * (UNITS - 1))]
        pltpu.make_async_copy(gone, gone, send_sems.at[0]).wait()

        @pl.when(stays)
        def _():
            gone = send2.at[pl.ds(0, 32 * (PENCIL - 1))]
            pltpu.make_async_copy(gone, gone, send_sems.at[1]).wait()

        @pl.when(jnp.logical_not(stays))
        def _():
            pltpu.make_async_copy(send2, send2, send_sems.at[1]).wait()

    @pl.when(jnp.logical_not(works_y))
    def _():
        pltpu.make_async_copy(send1, send1, send_sems.at[0]).wait()

    @pl.when(works_z)
    def _():
        gone = send3.at[pl.ds(0, 32 * (SLAB - 1))]
        pltpu.make_async_copy(gone, gone, send_sems.at[2]).wait()


def per_device(strain, labels, moduli):
    consts = [jnp.asarray(const) for const in tables()]
    moduli, strain, labels, *consts = [
        pltpu.with_memory_space_constraint(x, pltpu.HBM) for x in (moduli, strain, labels, *consts)
    ]
    anywhere = pl.BlockSpec(memory_space=pltpu.HBM)
    return pl.pallas_call(
        kernel,
        out_shape=jax.ShapeDtypeStruct((COMPS, 2, MODES, 16, 128), F32),
        in_specs=[anywhere] * 9,
        out_specs=pl.BlockSpec(memory_space=pltpu.VMEM),
        scratch_shapes=[
            pltpu.SMEM((2, NPHASE), F32),
            pltpu.VMEM((COMPS, XW, 16, 128), BF16),
            pltpu.VMEM((XW, 16, 128), jnp.int32),
            pltpu.VMEM((2 * NY, 2 * NY), BF16),
            pltpu.VMEM((512, 512), BF16),
            pltpu.VMEM((2, 16, 128), F32),
            pltpu.VMEM((256, 256), BF16),
            pltpu.VMEM((2, 16, 128), F32),
            pltpu.VMEM((2, 8, 128), F32),
            pltpu.VMEM((XW, 16, 128), F32),
            pltpu.VMEM((32 * UNITS, 128), BF16),
            pltpu.VMEM((32 * PENCIL, 128), BF16),
            pltpu.VMEM((32 * PENCIL, 128), BF16),
            pltpu.VMEM((32 * SLAB, 128), BF16),
            pltpu.VMEM((32 * SLAB, 128), BF16),
            pltpu.VMEM((32 * UNITS, 128), BF16),
            pltpu.SemaphoreType.DMA((3,)),
            pltpu.SemaphoreType.DMA((6,)),
            pltpu.SemaphoreType.DMA((3,)),
            pltpu.SemaphoreType.DMA((4,)),
        ],
        compiler_params=pltpu.CompilerParams(
            collective_id=0, has_side_effects=True, vmem_limit_bytes=32 * 1024 * 1024
        ),
    )(moduli, strain, labels, *consts)


def solution(mesh):
    return jax.shard_map(
        per_device,
        mesh=mesh,
        in_specs=(P(None, None, "pencil", "slab"), P(None, "pencil", "slab"), P()),
        out_specs=P(None, None, None, "pencil", "slab"),
        check_vma=False,
    )
```

```python
import math

import jax
import jax.numpy as jnp
import numpy as np
from jax import lax
from jax.experimental import pallas as pl
from jax.experimental.pallas import tpu as pltpu
from jax.sharding import PartitionSpec as P

MESH = pl.DeviceIdType.MESH
NX, NY, NZ = 2048, 512, 2048
XW, MODES, KX0, NPHASE, COMPS = 16, 2, 64, 4, 6
PENCIL, SLAB = 32, 16
UNITS = 12
Y_PLACES = (0, 2, 5, 7, 8, 10, 13, 15, 24, 26, 29, 31)
SLAB_ORDER = (0, 1, 2, 3, 4, 5, 14, 15, 6, 7, 12, 13, 8, 9, 10, 11)
Q_FLOOR = 0.01
F32, BF16 = jnp.float32, jnp.bfloat16


def wrap(index, size):
    return jnp.where(index >= size, index - size, index)


def z_place(unit, owner):
    return wrap(wrap(unit + 5 * owner % UNITS, UNITS) + SLAB - 4, SLAB)


def z_unit(place, owner):
    return lax.rem(wrap(place + 4, SLAB) + 13 * UNITS - 5 * owner, UNITS)


def far_first(chips, each):
    order = sorted(range(chips), key=lambda step: -min(step, chips - step))
    return [chip * each + i for chip in order for i in reversed(range(each))]


def parts_table(angle):
    cosine, sine = np.cos(angle), np.sin(angle)
    return np.stack([np.stack([cosine, sine], 1), np.stack([-sine, cosine], 1)])


def tables():
    angle = 2 * math.pi / NY * (np.outer(np.arange(NY), np.arange(NY)) % NY)
    along_y = parts_table(angle).reshape(2, PENCIL, 16, 2, PENCIL, 16)
    along_y = along_y.transpose(1, 0, 2, 4, 3, 5).reshape(2 * NY, 2 * NY)
    angle = 2 * math.pi / 16 * (np.outer(np.arange(16), np.arange(16)) % 16)
    coarse = np.einsum("obrs,kj->okbsrj", np.roll(parts_table(angle), 4, 3), np.eye(16)).reshape(512, 512)
    angle = 2 * math.pi / NZ * np.outer(np.arange(16), np.arange(128))
    turn = np.stack([np.cos(angle), np.sin(angle)]) / math.sqrt(NZ)
    angle = 2 * math.pi / 128 * (np.outer(np.arange(128), np.arange(128)) % 128)
    fine = parts_table(angle).reshape(2, SLAB, 8, 256)[:, list(SLAB_ORDER)].transpose(1, 0, 2, 3)
    fine = fine.reshape(256, 256)
    angle = math.pi / NY * np.arange(NY).reshape(PENCIL, 16, 1)
    angle = np.broadcast_to(angle, (PENCIL, 16, 128))
    freq_y = np.stack([np.sin(angle), np.cos(angle)], 1)
    angle = math.pi / NZ * np.arange(NZ).reshape(SLAB, 1, 128)
    angle = np.broadcast_to(angle, (SLAB, 8, 128))
    freq_z = np.stack([np.sin(angle), np.cos(angle)], 1)
    return (
        along_y.astype(BF16),
        coarse.astype(BF16),
        turn.astype(np.float32),
        fine.astype(BF16),
        freq_y.astype(np.float32),
        freq_z.astype(np.float32),
    )


def turn_z(mixed, turn):
    mixed = mixed.reshape(2, 16, 16, 128)
    cosine, sine = turn[0][None], turn[1][None]
    real = mixed[0] * cosine + mixed[1] * sine
    imag = mixed[1] * cosine - mixed[0] * sine
    parts = [part.reshape(256, 128).astype(BF16) for part in (real, imag)]
    return jnp.concatenate(parts, 1)


def exchange_bit(values, axis, bit):
    size = values.shape[axis]
    if 2 * bit == size:
        return pltpu.roll(values, bit, axis)
    index = lax.broadcasted_iota(jnp.int32, values.shape, axis)
    return jnp.where((index & bit) != 0, pltpu.roll(values, bit, axis), pltpu.roll(values, size - bit, axis))


def last_points(band, fine):
    product = lax.dot_general(fine[...], band, (((1,), (1,)), ((), ())), preferred_element_type=F32)
    halves = []
    for half in range(2):
        values = product[:, 128 * half : 128 * half + 128].reshape(32, 8, 128)
        row = lax.broadcasted_iota(jnp.int32, values.shape, 1)
        block = lax.broadcasted_iota(jnp.int32, values.shape, 2) // 16
        for bit in (1, 2, 4):
            traded = exchange_bit(exchange_bit(values, 1, bit), 2, 16 * bit)
            values = jnp.where(((row ^ block) & bit) == 0, values, traded)
        halves.append(values.reshape(256, 128))
    return jnp.concatenate(halves, 1)


def contrast(labels, values, base, factor):
    levels = [(values[phase] - base) * factor for phase in range(NPHASE)]
    chosen = jnp.where(labels == 2, levels[2], levels[3])
    chosen = jnp.where(labels == 1, levels[1], chosen)
    return jnp.where(labels == 0, levels[0], chosen)


def wave(mode, plane):
    angle = 2 * math.pi / NX * ((KX0 + mode) * plane % NX)
    scale = 1 / math.sqrt(XW)
    return float(math.cos(angle) * scale), float(-math.sin(angle) * scale)


def kernel(
    moduli_hbm,
    strain_hbm,
    labels_hbm,
    along_y_hbm,
    coarse_hbm,
    turn_hbm,
    fine_hbm,
    freq_y_hbm,
    freq_z_hbm,
    out,
    moduli,
    strain,
    labels,
    along_y,
    coarse,
    turn,
    fine,
    freq_y,
    freq_z,
    shear,
    send1,
    land1,
    send2,
    land2,
    send3,
    land3,
    in_sems,
    table_sems,
    send_sems,
    land_sems,
):
    pencil = lax.axis_index("pencil")
    slab = lax.axis_index("slab")
    unit_y = sum(jnp.where(pencil == place, unit, 0) for unit, place in enumerate(Y_PLACES))
    works_y = sum(jnp.where(pencil == place, 1, 0) for place in Y_PLACES) > 0
    works_z = wrap(slab + 4, SLAB) < UNITS

    barrier = pltpu.get_barrier_semaphore()

    @pl.when(works_z)
    def _():
        for step in far_first(8, 2)[:-1]:
            other = wrap(slab + step, SLAB)
            pl.semaphore_signal(barrier, inc=1, device_id=(pencil, other), device_id_type=MESH)

    @pl.when(works_y)
    def _():
        for step in far_first(8, 4)[:-1]:
            other = wrap(pencil + step, PENCIL)
            pl.semaphore_signal(barrier, inc=1, device_id=(other, slab), device_id_type=MESH)

    moduli_load = pltpu.make_async_copy(moduli_hbm, moduli, in_sems.at[2])
    moduli_load.start()
    loads = [
        pltpu.make_async_copy(strain_hbm, strain, in_sems.at[0]),
        pltpu.make_async_copy(labels_hbm, labels, in_sems.at[1]),
    ]
    for load in loads:
        load.start()
    pairs = [
        (freq_y_hbm.at[pencil], freq_y),
        (freq_z_hbm.at[slab], freq_z),
        (along_y_hbm, along_y),
        (coarse_hbm, coarse),
        (turn_hbm, turn),
        (fine_hbm, fine),
    ]
    table_loads = [pltpu.make_async_copy(a, b, table_sems.at[i]) for i, (a, b) in enumerate(pairs)]
    for load in table_loads:
        load.start()

    moduli_load.wait()
    lam0 = 0.5 * (
        jnp.minimum(jnp.minimum(moduli[0, 0], moduli[0, 1]), jnp.minimum(moduli[0, 2], moduli[0, 3]))
        + jnp.maximum(jnp.maximum(moduli[0, 0], moduli[0, 1]), jnp.maximum(moduli[0, 2], moduli[0, 3]))
    )
    mu0 = 0.5 * (
        jnp.minimum(jnp.minimum(moduli[1, 0], moduli[1, 1]), jnp.minimum(moduli[1, 2], moduli[1, 3]))
        + jnp.maximum(jnp.maximum(moduli[1, 0], moduli[1, 1]), jnp.maximum(moduli[1, 2], moduli[1, 3]))
    )

    for load in loads:
        load.wait()

    def emit(comp, mode, real, imag):
        start = 32 * (2 * comp + mode)
        send1[start : start + 16, :] = real.astype(BF16)
        send1[start + 16 : start + 32, :] = imag.astype(BF16)

    def add(total, term):
        return term if total is None else total + term

    level_lam = [moduli[0, phase] for phase in range(NPHASE)]
    level_mu = [moduli[1, phase] for phase in range(NPHASE)]
    shared = [[None, None] for _ in range(MODES)]
    sums = [[[None, None] for _ in range(MODES)] for _ in range(3)]
    for plane in range(XW):
        phases = labels[plane]
        shift_lam = contrast(phases, level_lam, lam0, 1.0)
        shift_mu = contrast(phases, level_mu, mu0, 2.0)
        shear[plane] = shift_mu
        parts = [strain[comp, plane].astype(F32) for comp in range(3)]
        trace = shift_lam * (parts[0] + parts[1] + parts[2])
        parts = [shift_mu * part for part in parts]
        for mode in range(MODES):
            for side, weight in enumerate(wave(mode, plane)):
                if weight == 0.0:
                    continue
                shared[mode][side] = add(shared[mode][side], weight * trace)
                for comp in range(3):
                    sums[comp][mode][side] = add(sums[comp][mode][side], weight * parts[comp])
    for comp in range(3):
        for mode in range(MODES):
            emit(comp, mode, sums[comp][mode][0] + shared[mode][0], sums[comp][mode][1] + shared[mode][1])
    sums = [[[None, None] for _ in range(MODES)] for _ in range(3)]
    for plane in range(XW):
        shift_mu = shear[plane]
        parts = [shift_mu * strain[3 + comp, plane].astype(F32) for comp in range(3)]
        for mode in range(MODES):
            for side, weight in enumerate(wave(mode, plane)):
                if weight == 0.0:
                    continue
                for comp in range(3):
                    sums[comp][mode][side] = add(sums[comp][mode][side], weight * parts[comp])
    for comp in range(3):
        for mode in range(MODES):
            emit(3 + comp, mode, sums[comp][mode][0], sums[comp][mode][1])

    greetings = jnp.where(works_y, UNITS - 1, UNITS) + jnp.where(works_z, UNITS - 1, UNITS)
    pl.semaphore_wait(barrier, greetings)

    def tile(index):
        return pl.ds(pl.multiple_of(index * 32, 32), 32)

    for unit in (7, 6, 11, 10, 5, 4, 9, 8, 3, 2, 1, 0):
        place = Y_PLACES[unit]

        @pl.when(pencil != place)
        def _():
            pltpu.make_async_remote_copy(
                src_ref=send1.at[tile(unit)],
                dst_ref=land1.at[tile(pencil)],
                send_sem=send_sems.at[0],
                recv_sem=land_sems.at[0],
                device_id=(place, slab),
                device_id_type=MESH,
            ).start()

    @pl.when(works_y)
    def _():
        pltpu.make_async_copy(send1.at[tile(unit_y)], land1.at[tile(pencil)], land_sems.at[0]).start()

    for load in table_loads[:2]:
        load.wait()
    sin_y, cos_y = freq_y[0], freq_y[1]
    sin_z, cos_z = (jnp.tile(freq_z[i], (2, 1)) for i in range(2))
    cos_yz, sin_cos, cos_sin = cos_y * cos_z, sin_y * cos_z, cos_y * sin_z

    arrival = jnp.where(wrap(slab + 4, SLAB) < SLAB // 2, 1, 3)

    def exchange_2(owner, own):
        mine = z_place(unit_y, owner)
        source = send2.at[tile(owner)]
        target = land2.at[tile(wrap(slab + 4, SLAB))]
        if own:
            pltpu.make_async_copy(source, target, land_sems.at[arrival]).start()
        else:
            pltpu.make_async_remote_copy(
                src_ref=source,
                dst_ref=target,
                send_sem=send_sems.at[1],
                recv_sem=land_sems.at[arrival],
                device_id=(owner, mine),
                device_id_type=MESH,
            ).start()

    stays = works_z & (z_unit(slab, pencil) == unit_y)

    @pl.when(works_y)
    def _():
        table_loads[2].wait()
        pltpu.make_async_copy(land1, land1, land_sems.at[0]).wait()
        for begin, end in ((0, 4), (4, 8), (8, 16), (16, 24), (24, 32)):
            rows = slice(32 * begin, 32 * end)
            band = jnp.dot(along_y[rows, :], land1[...], preferred_element_type=F32)
            send2[rows, :] = (band * (1 / math.sqrt(NY))).astype(BF16)
            for owner in range(begin, end):
                if owner not in Y_PLACES:
                    exchange_2(owner, False)
                    continue
                own = stays & (pencil == owner)

                @pl.when(own)
                def _():
                    exchange_2(owner, True)

                @pl.when(jnp.logical_not(own))
                def _():
                    exchange_2(owner, False)

    for load in table_loads[3:]:
        load.wait()

    @pl.when(jnp.logical_not(works_y))
    def _():
        table_loads[2].wait()

    @pl.when(works_z)
    def _():
        unit = z_unit(slab, pencil)
        mixed = None
        for slabs, arrived in ((slice(0, 256), 1), (slice(256, 512), 3)):
            pltpu.make_async_copy(land2.at[slabs], land2.at[slabs], land_sems.at[arrived]).wait()
            part = jnp.dot(coarse[:, slabs], land2[slabs, :], preferred_element_type=F32)
            mixed = part if mixed is None else mixed + part
        band = turn_z(mixed, turn)
        points = last_points(band, fine)
        for place, owner in enumerate(SLAB_ORDER):
            for part in range(2):
                row, start = 16 * place + 8 * part, 32 * owner + 16 * part
                halves = [points[row : row + 8, 128 * half : 128 * half + 128] for half in range(2)]
                send3[start : start + 16, :] = jnp.concatenate(halves, 0).astype(BF16)
        for owner in SLAB_ORDER:
            source, target = send3.at[tile(owner)], land3.at[tile(unit)]

            @pl.when(slab == owner)
            def _():
                pltpu.make_async_copy(source, target, land_sems.at[2]).start()

            @pl.when(slab != owner)
            def _():
                pltpu.make_async_remote_copy(
                    src_ref=source,
                    dst_ref=target,
                    send_sem=send_sems.at[2],
                    recv_sem=land_sems.at[2],
                    device_id=(pencil, owner),
                    device_id_type=MESH,
                ).start()

    factor = (lam0 + mu0) / (mu0 * (lam0 + 2.0 * mu0))
    half_mu = 1.0 / (2.0 * mu0)
    weights = []
    for mode in range(MODES):
        angle = math.pi / NX * (KX0 + mode)
        sin_x, cos_x = math.sin(angle), math.cos(angle)
        qx, qy, qz = sin_x * cos_yz, cos_x * sin_cos, cos_x * cos_sin
        inverse = 1.0 / jnp.maximum(qx * qx + qy * qy + qz * qz, Q_FLOOR)
        weights.append((qx, qy, qz, half_mu * inverse, factor * inverse * inverse))
    pltpu.make_async_copy(land3, land3, land_sems.at[2]).wait()
    for mode in range(MODES):
        qx, qy, qz, first, second = weights[mode]
        for part in range(2):
            spectrum = []
            for comp in range(COMPS):
                start = 32 * (2 * comp + mode) + 16 * part
                spectrum.append(land3[start : start + 16, :].astype(F32))
            txx, tyy, tzz, tyz, txz, txy = spectrum
            vecx = txx * qx + txy * qy + txz * qz
            vecy = txy * qx + tyy * qy + tyz * qz
            vecz = txz * qx + tyz * qy + tzz * qz
            inner = second * (qx * vecx + qy * vecy + qz * vecz)
            vecx, vecy, vecz = first * vecx, first * vecy, first * vecz
            out[0, part, mode] = qx * (inner * qx - 2.0 * vecx)
            out[1, part, mode] = qy * (inner * qy - 2.0 * vecy)
            out[2, part, mode] = qz * (inner * qz - 2.0 * vecz)
            out[3, part, mode] = inner * qy * qz - (qy * vecz + qz * vecy)
            out[4, part, mode] = inner * qx * qz - (qx * vecz + qz * vecx)
            out[5, part, mode] = inner * qx * qy - (qx * vecy + qy * vecx)

    @pl.when(works_y)
    def _():
        gone = send1.at[pl.ds(0, 32 * (UNITS - 1))]
        pltpu.make_async_copy(gone, gone, send_sems.at[0]).wait()

        @pl.when(stays)
        def _():
            gone = send2.at[pl.ds(0, 32 * (PENCIL - 1))]
            pltpu.make_async_copy(gone, gone, send_sems.at[1]).wait()

        @pl.when(jnp.logical_not(stays))
        def _():
            pltpu.make_async_copy(send2, send2, send_sems.at[1]).wait()

    @pl.when(jnp.logical_not(works_y))
    def _():
        pltpu.make_async_copy(send1, send1, send_sems.at[0]).wait()

    @pl.when(works_z)
    def _():
        gone = send3.at[pl.ds(0, 32 * (SLAB - 1))]
        pltpu.make_async_copy(gone, gone, send_sems.at[2]).wait()


def per_device(strain, labels, moduli):
    consts = [jnp.asarray(const) for const in tables()]
    moduli, strain, labels, *consts = [
        pltpu.with_memory_space_constraint(x, pltpu.HBM) for x in (moduli, strain, labels, *consts)
    ]
    anywhere = pl.BlockSpec(memory_space=pltpu.HBM)
    return pl.pallas_call(
        kernel,
        out_shape=jax.ShapeDtypeStruct((COMPS, 2, MODES, 16, 128), F32),
        in_specs=[anywhere] * 9,
        out_specs=pl.BlockSpec(memory_space=pltpu.VMEM),
        scratch_shapes=[
            pltpu.SMEM((2, NPHASE), F32),
            pltpu.VMEM((COMPS, XW, 16, 128), BF16),
            pltpu.VMEM((XW, 16, 128), jnp.int32),
            pltpu.VMEM((2 * NY, 2 * NY), BF16),
            pltpu.VMEM((512, 512), BF16),
            pltpu.VMEM((2, 16, 128), F32),
            pltpu.VMEM((256, 256), BF16),
            pltpu.VMEM((2, 16, 128), F32),
            pltpu.VMEM((2, 8, 128), F32),
            pltpu.VMEM((XW, 16, 128), F32),
            pltpu.VMEM((32 * UNITS, 128), BF16),
            pltpu.VMEM((32 * PENCIL, 128), BF16),
            pltpu.VMEM((32 * PENCIL, 128), BF16),
            pltpu.VMEM((32 * SLAB, 128), BF16),
            pltpu.VMEM((32 * SLAB, 128), BF16),
            pltpu.VMEM((32 * UNITS, 128), BF16),
            pltpu.SemaphoreType.DMA((3,)),
            pltpu.SemaphoreType.DMA((6,)),
            pltpu.SemaphoreType.DMA((3,)),
            pltpu.SemaphoreType.DMA((4,)),
        ],
        compiler_params=pltpu.CompilerParams(
            collective_id=0, has_side_effects=True, vmem_limit_bytes=32 * 1024 * 1024
        ),
    )(moduli, strain, labels, *consts)


def solution(mesh):
    return jax.shard_map(
        per_device,
        mesh=mesh,
        in_specs=(P(None, None, "pencil", "slab"), P(None, "pencil", "slab"), P()),
        out_specs=P(None, None, None, "pencil", "slab"),
        check_vma=False,
    )
```
